32 devices in a mesh: row: 4 (over y, core), col: 8 (over z, x).
Axes of the slice: x: 2, y: 2, z: 4, core: 2. Of those that a mesh axis runs over, the one named last changes fastest.
Arguments:
- noise_latents: bfloat16 [4096, 2048], P('row', 'col'), may hold values from -40 to 40
- data_latents: bfloat16 [16384, 2048], P('col', 'row'), may hold values from -6 to 6
- noise_sizes: int32 [8], replicated, may hold values from 1 to 1024, 4096 in all
- data_sizes: int32 [8], replicated, may hold values from 1 to 4096, 16384 in all
Outputs:
- velocity: float32 [4096, 2048], P('row', 'col')
- noise_potential: float32 [4096], P('row')
- data_potential: float32 [16384], P('col')
The draws below stay inside these ranges and needn't reach their ends.
Inputs may be any that keep to these rules, and one draw needn't show every extreme that they name: `noise_sizes`: clusters take consecutive runs of noise samples in order of the cluster number; every cluster is non-empty and the largest holds exactly 1024. `data_sizes`: clusters take consecutive runs of data samples in order of the cluster number; every cluster is non-empty and the largest holds exactly 4096.
All inputs are finite; a program needn't handle non-finite values.
Results may differ from the reference program's by a relative error of at most 0.007.
Values may be sent and summed in bfloat16 or wider, within the bound.
A program may use at most 128 MiB of HBM per device.

```python
import math
import jax
import jax.numpy as jnp
import numpy as np
from jax import lax

W = 2048
COLS_DEV = 2048
CLUSTERS = 8
ITERS = 3
NN = 4096
ND = 16384
N_COL = 8


def draw_noise_latents(key, part):
    key = jax.random.fold_in(key, 11)
    gauss_key = jax.random.fold_in(key, 0)
    gaussian = jax.random.normal(gauss_key, (NN, W), jnp.float32)
    return jnp.clip(gaussian, -6.0, 6.0).astype(jnp.bfloat16)


def block_scale(own_key, extent, cuts, low, high):
    def one(dim, parts):
        steps = jax.random.uniform(jax.random.fold_in(jax.random.fold_in(own_key, 6), dim), (parts,), jnp.float32, low / len(cuts), high / len(cuts))
        return jnp.repeat(jnp.exp(steps), extent[dim] // parts).reshape((-1,) + (1,) * (len(extent) - dim - 1))

    level = one(*cuts[0])
    for cut in cuts[1:]:
        level = level * one(*cut)
    return level


def length_profile(count, total, limit, slope):
    portions = [(1 << 20) // math.isqrt(grade ** slope) + 1 for grade in range(2, count + 1)]
    surplus, given = total - limit - (count - 1), [1] * (count - 1)
    while surplus > 0:
        free = [i for i in range(count - 1) if given[i] < limit]
        pool, left = sum([portions[i] for i in free]), surplus
        for i in free:
            addition = min(limit - given[i], max(1, left * portions[i] // pool), surplus)
            given[i] = given[i] + addition
            surplus = surplus - addition
    return np.array([limit] + given)


def ragged(stream_key, count, total, limit, skew):
    if count == 2:
        one = jax.random.randint(stream_key, (), max(1, total - limit), min(limit, total - 1) + 1)
        return jnp.stack([one, total - one])
    sizes = jnp.asarray(length_profile(count, total, limit, skew), jnp.int32)
    twos = (count - 1) // 2
    giver, sink = sizes[1:1 + 2 * twos:2], sizes[2:2 + 2 * twos:2]
    margin = jnp.minimum(giver - 1, limit - sink)
    passed = jax.random.randint(jax.random.fold_in(stream_key, 1), (twos,), 0, 1 << 20) % (margin + 1)
    sizes = sizes.at[1:1 + 2 * twos:2].set(giver - passed).at[2:2 + 2 * twos:2].set(sink + passed)
    return sizes[jax.random.permutation(jax.random.fold_in(stream_key, 2), count)]


def bell_draw(own_key, shape, spread, bound, cuts=(), kind=jnp.bfloat16):
    drawn = jax.random.normal(own_key, shape, jnp.float32) * spread
    if len(cuts) > 0:
        drawn = block_scale(own_key, shape, cuts, -0.22, 0.18) * drawn
    return jnp.clip(drawn, min=-bound, max=bound).astype(kind)


def setup_inputs(seed: int = 0) -> dict:
    seeds = jax.random.split(jax.random.key(seed), 5)
    noise_latents = draw_noise_latents(jax.random.fold_in(seeds[4], 71), 0)
    data_latents = bell_draw(seeds[1], (ND, W), 1.0, 6.0, ((0, 8), (1, 4)))
    noise_sizes = ragged(seeds[2], CLUSTERS, NN, NN // 4, 2).astype(jnp.int32)
    data_sizes = ragged(seeds[3], CLUSTERS, ND, ND // 4, 2).astype(jnp.int32)
    return {"noise_latents": noise_latents, "data_latents": data_latents, "noise_sizes": noise_sizes, "data_sizes": data_sizes}


epsilon = 0.05
masked_value = -1e30


def cluster_of(positions, cluster_sizes):
    boundaries = jnp.cumsum(cluster_sizes).astype(jnp.int32)[:-1]
    return jnp.sum((positions[:, None] >= boundaries[None, :]).astype(jnp.int32), axis=1)


def masked_lse(scores, same_cluster, reduce_axis):
    masked = jnp.where(same_cluster, scores, masked_value)
    largest = jnp.max(masked, axis=reduce_axis, keepdims=True)
    totals = jnp.sum(jnp.where(same_cluster, jnp.exp(masked - largest), 0.0), axis=reduce_axis, keepdims=True)
    return jnp.squeeze(largest + jnp.log(totals), reduce_axis)


def reference(noise_latents, data_latents, noise_sizes, data_sizes):
    full_width = noise_latents.shape[1]
    row_block = math.gcd(NN, 512)
    noise_sq = jnp.sum(jnp.square(noise_latents.astype(jnp.float32)), axis=1)
    data_sq = jnp.sum(jnp.square(data_latents.astype(jnp.float32)), axis=1)
    blocks = noise_latents.reshape(NN // row_block, row_block, full_width)
    data_turned = data_latents.T

    def inner_block(block_rows):
        return jnp.dot(block_rows, data_turned, preferred_element_type=jnp.float32)

    inner = lax.map(inner_block, blocks).reshape(NN, ND)
    cost = (noise_sq[:, None] + data_sq[None, :] - 2.0 * inner) / full_width
    noise_cluster = cluster_of(jnp.arange(NN, dtype=jnp.int32), noise_sizes)
    data_cluster = cluster_of(jnp.arange(ND, dtype=jnp.int32), data_sizes)
    same_cluster = noise_cluster[:, None] == data_cluster[None, :]
    data_potential = jnp.zeros((ND,), jnp.float32)
    noise_potential = jnp.zeros((NN,), jnp.float32)
    for iteration in range(ITERS):
        noise_potential = -epsilon * masked_lse((data_potential[None, :] - cost) / epsilon, same_cluster, 1)
        data_potential = -epsilon * masked_lse((noise_potential[:, None] - cost) / epsilon, same_cluster, 0)
    scores = (data_potential[None, :] - cost) / epsilon
    row_lse = masked_lse(scores, same_cluster, 1)
    weights = jnp.where(same_cluster, jnp.exp(jnp.where(same_cluster, scores, masked_value) - row_lse[:, None]), 0.0)
    weights = weights.astype(jnp.bfloat16).reshape(NN // row_block, row_block, N_COL, COLS_DEV)
    data_blocks = data_latents.astype(jnp.float32).reshape(N_COL, COLS_DEV, full_width)

    def target_block(weight_rows):
        partials = jnp.einsum("rbk,bkw->rbw", weight_rows.astype(jnp.float32), data_blocks, precision=lax.Precision.HIGHEST)
        rounded = lax.optimization_barrier(partials.astype(jnp.bfloat16)).astype(jnp.float32)
        return jnp.sum(rounded, axis=1)

    target = lax.map(target_block, weights).reshape(NN, full_width)
    velocity = target - noise_latents.astype(jnp.float32)
    return (velocity, noise_potential, data_potential)
```

```python
import functools
import math

import jax
import jax.numpy as jnp
from jax import lax
from jax.experimental import pallas as pl
from jax.experimental.pallas import tpu as pltpu
from jax.sharding import PartitionSpec as P

ITERS = 3
EPSILON = 0.05
MASKED = -1e30
Z = 4
CORES = 2
PIECES = 4
T = 128
UNIT = EPSILON * math.log(2.0)
MESH = pl.DeviceIdType.MESH


def kernel(
    R, C, xin, yin, nsz, dsz,
    target, fout, gout,
    X, Y, S, Wt, NC, F, avec, bvec, qvec, nvec, cbuf, rbuf,
    psend, pown, xrecv, zsend, zrecv,
    local_sem, xg_send, xg_recv, yg_send, yg_recv,
    ce_send, ce_recv, re_send, re_recv, px_send, px_recv, pz_send, pz_recv,
):
    rows, wc = xin.shape
    cols, wr = yin.shape
    width = wc * C
    XN = C // Z
    YN = R // CORES
    r = lax.axis_index("row")
    c = lax.axis_index("col")
    z, x = lax.div(c, XN), lax.rem(c, XN)
    y, core = lax.div(r, CORES), lax.rem(r, CORES)
    scale = 2.0 / (width * UNIT)

    def rdma(src, dst, send, recv, **peer):
        return pltpu.make_async_remote_copy(
            src_ref=src, dst_ref=dst, send_sem=send, recv_sem=recv,
            device_id=peer, device_id_type=MESH,
        )

    barrier = pltpu.get_barrier_semaphore()
    for k in range(1, C):
        pl.semaphore_signal(barrier, inc=1, device_id={"col": lax.rem(c + k, C)}, device_id_type=MESH)
    for k in range(1, R):
        pl.semaphore_signal(barrier, inc=1, device_id={"row": lax.rem(r + k, R)}, device_id_type=MESH)
    pl.semaphore_wait(barrier, C - 1 + R - 1)

    sent = []

    def noise_part(block):
        return X.at[:, pl.ds(pl.multiple_of(block * wc, wc), wc)]

    def noise_copy(block, way, own=False):
        peer = {0: c + XN, 1: c - XN, 2: c + 1, 3: c - 1}[way]
        return rdma(xin if own else noise_part(block), noise_part(block),
                    xg_send.at[block, way], xg_recv.at[block], col=peer)

    def can_noise(way):
        return {0: z + 1 < Z, 1: z >= 1, 2: x + 1 < XN, 3: x >= 1}[way]

    def send(cond, make):
        pl.when(cond)(lambda: make().start())
        sent.append((cond, make))

    def noise_send(block, way, cond=None, own=False):
        ok = can_noise(way) if cond is None else jnp.logical_and(cond, can_noise(way))
        send(ok, lambda: noise_copy(block, way, own))

    piece = cols // PIECES

    def data_part(block, q):
        return Y.at[pl.ds(q * piece, piece), pl.ds(pl.multiple_of(block * wr, wr), wr)]

    def data_copy(block, q, way, own=False):
        peer = {0: r + CORES, 1: r - CORES, 2: r + 1 - 2 * core}[way]
        src = yin.at[pl.ds(q * piece, piece), :] if own else data_part(block, q)
        return rdma(src, data_part(block, q), yg_send.at[block, q, way], yg_recv.at[block, q], row=peer)

    def can_data(way):
        return {0: y + 1 < YN, 1: y >= 1, 2: y >= 0}[way]

    def data_send(block, q, way, cond=None, own=False):
        ok = can_data(way) if cond is None else jnp.logical_and(cond, can_data(way))
        send(ok, lambda: data_copy(block, q, way, own))

    for way in (0, 1, 2, 3):
        noise_send(c, way, own=True)
    for q in range(PIECES):
        for way in (0, 1):
            data_send(r, q, way, own=True)
    for q in range(PIECES):
        data_send(r, q, 2, own=True)
    lx = pltpu.make_async_copy(xin, noise_part(c), local_sem.at[0])
    ly = pltpu.make_async_copy(yin, Y.at[:, pl.ds(pl.multiple_of(r * wr, wr), wr)], local_sem.at[1])
    lx.start()
    ly.start()

    def cluster(position, sizes):
        total = jnp.int32(0)
        number = jnp.zeros(position.shape, jnp.int32)
        for k in range(7):
            total = total + sizes[k]
            number = number + (position >= total).astype(jnp.int32)
        return number

    for i in range(rows // T):
        NC[pl.ds(i * T, T), :] = cluster(
            r * rows + i * T + lax.broadcasted_iota(jnp.int32, (T, T), 0), nsz)

    def take_noise(dz, dx):
        here = jnp.logical_and(
            jnp.logical_and(z + dz >= 0, z + dz < Z), jnp.logical_and(x + dx >= 0, x + dx < XN))
        block = c + dz * XN + dx
        pl.when(here)(lambda: noise_copy(block, 0).wait_recv())
        if dx == 0:
            noise_send(block, 1 if dz > 0 else 0, here)
            noise_send(block, 2, here)
            noise_send(block, 3, here)
        elif abs(dx) < XN - 1:
            noise_send(block, 3 if dx > 0 else 2, here)

    def take_data(dy, q):
        here = jnp.logical_and(y + dy >= 0, y + dy < YN)
        block = r + dy * CORES
        pl.when(here)(lambda: data_copy(block, q, 0).wait_recv())
        if abs(dy) < YN - 1:
            data_send(block, q, 1 if dy > 0 else 0, here)
        data_send(block, q, 2, here)

    def signs(d):
        return (d, -d) if d else (0,)

    for step in range(1, Z + 1):
        if step < Z:
            for dz in signs(step):
                take_noise(dz, 0)
        if step <= PIECES:
            for dy in signs(1):
                take_data(dy, step - 1)
        for dz in signs(step - 1):
            for dx in signs(1):
                take_noise(dz, dx)
    for step in range(2, XN):
        for dz in range(1 - Z, Z):
            for dx in signs(step):
                take_noise(dz, dx)
    for step in range(2, YN):
        for q in range(PIECES):
            for dy in signs(step):
                take_data(dy, q)
    sibling = r + 1 - 2 * core
    for dy in range(1 - YN, YN):
        here = jnp.logical_and(y + dy >= 0, y + dy < YN)
        for q in range(PIECES):
            pl.when(here)(lambda dy=dy, q=q: data_copy(sibling + dy * CORES, q, 0).wait_recv())
    lx.wait()
    ly.wait()

    def squares(ref, i):
        total = jnp.zeros((T, T), jnp.float32)
        for k in range(width // T):
            v = ref[pl.ds(pl.multiple_of(i * T, T), T), pl.ds(k * T, T)].astype(jnp.float32)
            total = total + v * v
        return jnp.sum(total.T, axis=0, keepdims=True) * (1.0 / (width * UNIT))

    def lanes(i, n=T):
        return pl.ds(pl.multiple_of(i * n, n), n)

    @pl.loop(0, cols // (2 * T))
    def _(j):
        both = lax.dot_general(
            X[...], Y[lanes(j, 2 * T), :], (((1,), (1,)), ((), ())), preferred_element_type=jnp.float32)
        for h in range(2):
            i = j * 2 + h
            dc = cluster(c * cols + i * T + lax.broadcasted_iota(jnp.int32, (1, T), 1), dsz)
            S[:, lanes(i)] = jnp.where(NC[...] == dc, both[:, h * T:(h + 1) * T] * scale, MASKED)
            q = squares(Y, i)
            qvec[:, lanes(i)] = q
            avec[:, lanes(i)] = -q

    @pl.loop(0, rows // T)
    def _(i):
        nvec[:, lanes(i)] = squares(X, i)

    def over_cols(e):
        @pl.loop(0, rows // T)
        def _(i):
            def term(k):
                return S[lanes(i), pl.ds(k * T, T)] + avec[:, pl.ds(k * T, T)]

            top = term(0)
            for k in range(1, cols // T):
                top = jnp.maximum(top, term(k))
            total = jnp.exp2(term(0) - top)
            for k in range(1, cols // T):
                total = total + jnp.exp2(term(k) - top)
            top, total = top.T, total.T
            best = jnp.max(top, axis=0, keepdims=True)
            cbuf[e, c, 0:1, lanes(i)] = best
            cbuf[e, c, 1:2, lanes(i)] = jnp.sum(total * jnp.exp2(top - best), axis=0, keepdims=True)

    def spread(vec):
        for i in range(rows // T):
            F[pl.ds(i * T, T), :] = jnp.broadcast_to(vec[:, i * T:(i + 1) * T], (T, T)).T

    def over_rows(e):
        G = 64

        @pl.loop(0, cols // T)
        def _(k):
            def term(i):
                return S[pl.ds(i * G, G), lanes(k)] + F[pl.ds(i * G, G), :]

            top = term(0)
            for i in range(1, rows // G):
                top = jnp.maximum(top, term(i))
            total = jnp.exp2(term(0) - top)
            for i in range(1, rows // G):
                total = total + jnp.exp2(term(i) - top)
            best = jnp.max(top, axis=0, keepdims=True)
            rbuf[e, r, 0:1, lanes(k)] = best
            rbuf[e, r, 1:2, lanes(k)] = jnp.sum(total * jnp.exp2(top - best), axis=0, keepdims=True)

    def exchange(buf, send_sem, recv_sem, e, me, n, axis):
        for k in range(1, n):
            rdma(buf.at[e, me], buf.at[e, me], send_sem.at[e, k - 1], recv_sem.at[e, me],
                 **{axis: lax.rem(me + k, n)}).start()
        for k in range(1, n):
            other = lax.rem(me + k, n)
            rdma(buf.at[e, other], buf.at[e, other], send_sem.at[e, k - 1], recv_sem.at[e, other],
                 **{axis: other}).wait_recv()
        best = buf[e, 0, 0:1, :]
        for k in range(1, n):
            best = jnp.maximum(best, buf[e, k, 0:1, :])
        total = buf[e, 0, 1:2, :] * jnp.exp2(buf[e, 0, 0:1, :] - best)
        for k in range(1, n):
            total = total + buf[e, k, 1:2, :] * jnp.exp2(buf[e, k, 0:1, :] - best)
        return best + jnp.log(total) * (1.0 / math.log(2.0))

    @pl.loop(0, ITERS)
    def _(e):
        over_cols(e)
        b = -exchange(cbuf, ce_send, ce_recv, e, c, C, "col")
        bvec[...] = b
        spread(b)
        over_rows(e)
        avec[...] = -exchange(rbuf, re_send, re_recv, e, r, R, "row")

    fout[...] = (bvec[...] + nvec[...]) * UNIT
    gout[...] = (avec[...] + qvec[...]) * UNIT
    over_cols(ITERS)
    spread(exchange(cbuf, ce_send, ce_recv, ITERS, c, C, "col"))

    @pl.loop(0, cols // T)
    def _(k):
        Wt[:, lanes(k)] = jnp.exp2(S[:, lanes(k)] + avec[:, lanes(k)] - F[...]).astype(jnp.bfloat16)

    def partial_sum(part):
        return jnp.dot(Wt[...], Y[:, lanes(part, wc)], preferred_element_type=jnp.float32).astype(jnp.bfloat16)

    def px_copy(k, d):
        return rdma(psend.at[k, d - 1], xrecv.at[k, d - 1], px_send.at[k, d - 1], px_recv.at[k, d - 1],
                    col=z * XN + lax.rem(x + d, XN))

    def pz_copy(k):
        return rdma(zsend.at[k], zrecv.at[k], pz_send.at[k], pz_recv.at[k],
                    col=lax.rem(z + 1 + k, Z) * XN + x)

    @pl.loop(0, Z)
    def _(k):
        zd = lax.rem(z + 1 + k, Z)
        for d in range(1, XN):
            psend[k, d - 1] = partial_sum(zd * XN + lax.rem(x + d, XN))
            px_copy(k, d).start()
        pown[k] = partial_sum(zd * XN + x)

    def x_sum(k):
        for d in range(1, XN):
            px_copy(k, d).wait_recv()
        total = pown[k].astype(jnp.float32)
        for d in range(1, XN):
            total = total + xrecv[k, d - 1].astype(jnp.float32)
        return total

    @pl.loop(0, Z - 1)
    def _(k):
        zsend[k] = x_sum(k).astype(jnp.bfloat16)
        pz_copy(k).start()

    total = x_sum(Z - 1)
    for k in range(Z - 1):
        pz_copy(k).wait_recv()
        total = total + zrecv[k].astype(jnp.float32)
    target[...] = total

    for cond, make in sent:
        pl.when(cond)(lambda make=make: make().wait_send())
    for e in range(ITERS + 1):
        for k in range(1, C):
            rdma(cbuf.at[e, c], cbuf.at[e, c], ce_send.at[e, k - 1], ce_recv.at[e, c],
                 col=lax.rem(c + k, C)).wait_send()
    for e in range(ITERS):
        for k in range(1, R):
            rdma(rbuf.at[e, r], rbuf.at[e, r], re_send.at[e, k - 1], re_recv.at[e, r],
                 row=lax.rem(r + k, R)).wait_send()
    for k in range(Z):
        for d in range(1, XN):
            px_copy(k, d).wait_send()
    for k in range(Z - 1):
        pz_copy(k).wait_send()


def per_device(R, C, noise_latents, data_latents, noise_sizes, data_sizes):
    rows, wc = noise_latents.shape
    cols, wr = data_latents.shape
    width = wc * C
    XN = C // Z
    f32, bf16 = jnp.float32, jnp.bfloat16
    dma = pltpu.SemaphoreType.DMA
    vmem = pl.BlockSpec(memory_space=pltpu.VMEM)
    anywhere = pl.BlockSpec(memory_space=pl.ANY)
    smem = pl.BlockSpec(memory_space=pltpu.SMEM)
    target, f, g = pl.pallas_call(
        functools.partial(kernel, R, C),
        out_shape=(
            jax.ShapeDtypeStruct((rows, wc), f32),
            jax.ShapeDtypeStruct((1, rows), f32),
            jax.ShapeDtypeStruct((1, cols), f32),
        ),
        in_specs=[anywhere, anywhere, smem, smem],
        out_specs=(vmem, vmem, vmem),
        scratch_shapes=[
            pltpu.VMEM((rows, width), bf16),
            pltpu.VMEM((cols, width), bf16),
            pltpu.VMEM((rows, cols), f32),
            pltpu.VMEM((rows, cols), bf16),
            pltpu.VMEM((rows, T), jnp.int32),
            pltpu.VMEM((rows, T), f32),
            pltpu.VMEM((1, cols), f32),
            pltpu.VMEM((1, rows), f32),
            pltpu.VMEM((1, cols), f32),
            pltpu.VMEM((1, rows), f32),
            pltpu.VMEM((ITERS + 1, C, 2, rows), f32),
            pltpu.VMEM((ITERS, R, 2, cols), f32),
            pltpu.VMEM((Z, XN - 1, rows, wc), bf16),
            pltpu.VMEM((Z, rows, wc), bf16),
            pltpu.VMEM((Z, XN - 1, rows, wc), bf16),
            pltpu.VMEM((Z - 1, rows, wc), bf16),
            pltpu.VMEM((Z - 1, rows, wc), bf16),
            dma((2,)),
            dma((C, 4)),
            dma((C,)),
            dma((R, PIECES, 3)),
            dma((R, PIECES)),
            dma((ITERS + 1, C - 1)),
            dma((ITERS + 1, C)),
            dma((ITERS, R - 1)),
            dma((ITERS, R)),
            dma((Z, XN - 1)),
            dma((Z, XN - 1)),
            dma((Z - 1,)),
            dma((Z - 1,)),
        ],
        compiler_params=pltpu.CompilerParams(
            collective_id=0, has_side_effects=True, vmem_limit_bytes=58 * 1024 * 1024
        ),
        name="sinkhorn",
    )(noise_latents, data_latents, noise_sizes, data_sizes)
    velocity = target - noise_latents.astype(f32)
    return velocity, f.reshape(rows), g.reshape(cols)


def solution(mesh):
    placed = (P("row", "col"), P("col", "row"), P(), P())
    return jax.shard_map(
        functools.partial(per_device, mesh.shape["row"], mesh.shape["col"]),
        mesh=mesh,
        in_specs=placed,
        out_specs=(P("row", "col"), P("row"), P("col")),
        check_vma=False,
    )
```

```python
import functools
import math

import jax
import jax.numpy as jnp
from jax import lax
from jax.experimental import pallas as pl
from jax.experimental.pallas import tpu as pltpu
from jax.sharding import PartitionSpec as P

ITERS = 3
EPSILON = 0.05
MASKED = -1e30
Z = 4
CORES = 2
PIECES = 4
T = 128
UNIT = EPSILON * math.log(2.0)
ORDER = ((3, 2, 1, 0), (3, 0, 2, 1), (0, 3, 1, 2), (0, 1, 2, 3))
MESH = pl.DeviceIdType.MESH


def kernel(
    R, C, xin, yin, nsz, dsz,
    target, fout, gout,
    X, Y, S, Pm, Wt, NC, F, Fb, avec, bvec, qvec, nvec, cfirst, rfirst, cbuf, rbuf,
    psend, pown, xrecv, zsend, zrecv,
    local_sem, xg_send, xg_recv, yg_send, yg_recv,
    cf_send, cf_recv, rf_send, rf_recv, ce_send, ce_recv, re_send, re_recv, px_send, px_recv, pz_send, pz_recv,
):
    rows, wc = xin.shape
    cols, wr = yin.shape
    width = wc * C
    XN = C // Z
    YN = R // CORES
    r = lax.axis_index("row")
    c = lax.axis_index("col")
    z, x = lax.div(c, XN), lax.rem(c, XN)
    y, core = lax.div(r, CORES), lax.rem(r, CORES)
    scale = 2.0 / (width * UNIT)

    def rdma(src, dst, send, recv, **peer):
        return pltpu.make_async_remote_copy(
            src_ref=src, dst_ref=dst, send_sem=send, recv_sem=recv,
            device_id=peer, device_id_type=MESH,
        )

    barrier = pltpu.get_barrier_semaphore()
    for k in range(1, C):
        pl.semaphore_signal(barrier, inc=1, device_id={"col": lax.rem(c + k, C)}, device_id_type=MESH)
    for k in range(1, R):
        pl.semaphore_signal(barrier, inc=1, device_id={"row": lax.rem(r + k, R)}, device_id_type=MESH)
    pl.semaphore_wait(barrier, C - 1 + R - 1)

    sent = []

    def noise_part(block):
        return X.at[:, pl.ds(pl.multiple_of(block * wc, wc), wc)]

    def noise_copy(block, way, own=False):
        peer = {0: c + XN, 1: c - XN, 2: c + 1, 3: c - 1}[way]
        return rdma(xin if own else noise_part(block), noise_part(block),
                    xg_send.at[block, way], xg_recv.at[block], col=peer)

    def can_noise(way):
        return {0: z + 1 < Z, 1: z >= 1, 2: x + 1 < XN, 3: x >= 1}[way]

    def send(cond, make):
        pl.when(cond)(lambda: make().start())
        sent.append((cond, make))

    def noise_send(block, way, cond=None, own=False):
        ok = can_noise(way) if cond is None else jnp.logical_and(cond, can_noise(way))
        send(ok, lambda: noise_copy(block, way, own))

    piece = cols // PIECES

    def data_part(block, q):
        return Y.at[pl.ds(q * piece, piece), pl.ds(pl.multiple_of(block * wr, wr), wr)]

    def data_copy(block, q, way, own=False):
        peer = {0: r + CORES, 1: r - CORES, 2: r + 1 - 2 * core}[way]
        src = yin.at[pl.ds(q * piece, piece), :] if own else data_part(block, q)
        return rdma(src, data_part(block, q), yg_send.at[block, q, way], yg_recv.at[block, q], row=peer)

    def can_data(way):
        return {0: y + 1 < YN, 1: y >= 1, 2: y >= 0}[way]

    def data_send(block, q, way, cond=None, own=False):
        ok = can_data(way) if cond is None else jnp.logical_and(cond, can_data(way))
        send(ok, lambda: data_copy(block, q, way, own))

    for way in (0, 1, 2, 3):
        noise_send(c, way, own=True)
    for q in range(PIECES):
        for way in (0, 1):
            data_send(r, q, way, own=True)
    for q in range(PIECES):
        data_send(r, q, 2, own=True)
    lx = pltpu.make_async_copy(xin, noise_part(c), local_sem.at[0])
    ly = pltpu.make_async_copy(yin, Y.at[:, pl.ds(pl.multiple_of(r * wr, wr), wr)], local_sem.at[1])
    lx.start()
    ly.start()

    def cluster(position, sizes):
        total = jnp.int32(0)
        number = jnp.zeros(position.shape, jnp.int32)
        for k in range(7):
            total = total + sizes[k]
            number = number + (position >= total).astype(jnp.int32)
        return number

    for i in range(rows // T):
        NC[pl.ds(i * T, T), :] = cluster(
            r * rows + i * T + lax.broadcasted_iota(jnp.int32, (T, T), 0), nsz)

    def take_noise(dz, dx):
        here = jnp.logical_and(
            jnp.logical_and(z + dz >= 0, z + dz < Z), jnp.logical_and(x + dx >= 0, x + dx < XN))
        block = c + dz * XN + dx
        pl.when(here)(lambda: noise_copy(block, 0).wait_recv())
        if dx == 0:
            noise_send(block, 1 if dz > 0 else 0, here)
            noise_send(block, 2, here)
            noise_send(block, 3, here)
        elif abs(dx) < XN - 1:
            noise_send(block, 3 if dx > 0 else 2, here)

    def take_data(dy, q):
        here = jnp.logical_and(y + dy >= 0, y + dy < YN)
        block = r + dy * CORES
        pl.when(here)(lambda: data_copy(block, q, 0).wait_recv())
        if abs(dy) < YN - 1:
            data_send(block, q, 1 if dy > 0 else 0, here)
        data_send(block, q, 2, here)

    def signs(d):
        return (d, -d) if d else (0,)

    for step in range(1, Z + 1):
        if step < Z:
            for dz in signs(step):
                take_noise(dz, 0)
        if step <= PIECES:
            for dy in signs(1):
                take_data(dy, step - 1)
        for dz in signs(step - 1):
            for dx in signs(1):
                take_noise(dz, dx)
    for step in range(2, XN):
        for dz in range(1 - Z, Z):
            for dx in signs(step):
                take_noise(dz, dx)
    for step in range(2, YN):
        for q in range(PIECES):
            for dy in signs(step):
                take_data(dy, q)
    sibling = r + 1 - 2 * core
    for dy in range(1 - YN, YN):
        here = jnp.logical_and(y + dy >= 0, y + dy < YN)
        for q in range(PIECES):
            pl.when(here)(lambda dy=dy, q=q: data_copy(sibling + dy * CORES, q, 0).wait_recv())
    lx.wait()
    ly.wait()

    def squares(ref, i):
        total = jnp.zeros((T, T), jnp.float32)
        for k in range(width // T):
            v = ref[pl.ds(pl.multiple_of(i * T, T), T), pl.ds(k * T, T)].astype(jnp.float32)
            total = total + v * v
        return jnp.sum(total.T, axis=0, keepdims=True) * (1.0 / (width * UNIT))

    def lanes(i, n=T):
        return pl.ds(pl.multiple_of(i * n, n), n)

    @pl.loop(0, cols // (2 * T))
    def _(j):
        both = lax.dot_general(
            X[...], Y[lanes(j, 2 * T), :], (((1,), (1,)), ((), ())), preferred_element_type=jnp.float32)
        for h in range(2):
            i = j * 2 + h
            dc = cluster(c * cols + i * T + lax.broadcasted_iota(jnp.int32, (1, T), 1), dsz)
            S[:, lanes(i)] = jnp.where(NC[...] == dc, both[:, h * T:(h + 1) * T] * scale, MASKED)
            q = squares(Y, i)
            qvec[:, lanes(i)] = q
            avec[:, lanes(i)] = -q

    def first_over_cols():
        @pl.loop(0, rows // T)
        def _(i):
            def term(k):
                return S[lanes(i), pl.ds(k * T, T)] + avec[:, pl.ds(k * T, T)]

            top = term(0)
            for k in range(1, cols // T):
                top = jnp.maximum(top, term(k))
            total = jnp.exp2(term(0) - top)
            for k in range(1, cols // T):
                total = total + jnp.exp2(term(k) - top)
            top, total = top.T, total.T
            best = jnp.max(top, axis=0, keepdims=True)
            cfirst[0, c, 0:1, lanes(i)] = best
            cfirst[0, c, 1:2, lanes(i)] = jnp.sum(total * jnp.exp2(top - best), axis=0, keepdims=True)

    def first_over_rows():
        G = 64

        @pl.loop(0, cols // T)
        def _(k):
            def term(i):
                return S[pl.ds(i * G, G), lanes(k)] + Fb[pl.ds(i * G, G), :]

            top = term(0)
            for i in range(1, rows // G):
                top = jnp.maximum(top, term(i))
            total = jnp.exp2(term(0) - top)
            for i in range(1, rows // G):
                total = total + jnp.exp2(term(i) - top)
            best = jnp.max(top, axis=0, keepdims=True)
            rfirst[0, r, 0:1, lanes(k)] = best
            rfirst[0, r, 1:2, lanes(k)] = jnp.sum(total * jnp.exp2(top - best), axis=0, keepdims=True)

    def over_cols(e, out):
        @pl.loop(0, rows // T)
        def _(i):
            b = Fb[lanes(i), :]
            total = jnp.zeros((T, T), jnp.float32)
            for k in range(cols // T):
                v = jnp.exp2(S[lanes(i), pl.ds(k * T, T)] + avec[:, pl.ds(k * T, T)] + b)
                out[lanes(i), pl.ds(k * T, T)] = v.astype(out.dtype)
                total = total + v
            cbuf[e, c, :, lanes(i)] = jnp.sum(total.T, axis=0, keepdims=True)

    def over_rows(e):
        G = 64

        @pl.loop(0, cols // T)
        def _(k):
            total = jnp.zeros((G, T), jnp.float32)
            for i in range(rows // G):
                total = total + Pm[pl.ds(i * G, G), lanes(k)] * F[pl.ds(i * G, G), :]
            rbuf[e, r, :, lanes(k)] = jnp.sum(total, axis=0, keepdims=True)

    def spread(vec, use):
        for i in range(rows // T):
            use(pl.ds(i * T, T), jnp.broadcast_to(vec[:, i * T:(i + 1) * T], (T, T)).T)

    def put(buf, send_sem, recv_sem, e, me, n, axis):
        return [
            rdma(buf.at[e, me], buf.at[e, me], send_sem.at[e, k - 1], recv_sem.at[e, me],
                 **{axis: lax.rem(me + k, n)})
            for k in range(1, n)
        ]

    def start(*group):
        for copy in put(*group):
            copy.start()

    def arrive(buf, send_sem, recv_sem, e, me, n, axis):
        for k in range(1, n):
            other = lax.rem(me + k, n)
            rdma(buf.at[e, other], buf.at[e, other], send_sem.at[e, k - 1], recv_sem.at[e, other],
                 **{axis: other}).wait_recv()

    def log2(v):
        return jnp.log(v) * (1.0 / math.log(2.0))

    def first_sum(buf, n):
        best = buf[0, 0, 0:1, :]
        for k in range(1, n):
            best = jnp.maximum(best, buf[0, k, 0:1, :])
        total = buf[0, 0, 1:2, :] * jnp.exp2(buf[0, 0, 0:1, :] - best)
        for k in range(1, n):
            total = total + buf[0, k, 1:2, :] * jnp.exp2(buf[0, k, 0:1, :] - best)
        return best + log2(total)

    def plain_sum(buf, e, n):
        total = buf[e, 0]
        for k in range(1, n):
            total = total + buf[e, k]
        return total

    cf = (cfirst, cf_send, cf_recv, 0, c, C, "col")
    rf = (rfirst, rf_send, rf_recv, 0, r, R, "row")

    def cg(e):
        return (cbuf, ce_send, ce_recv, e, c, C, "col")

    def rg(e):
        return (rbuf, re_send, re_recv, e, r, R, "row")

    first_over_cols()
    start(*cf)

    @pl.loop(0, rows // T)
    def _(i):
        nvec[:, lanes(i)] = squares(X, i)

    arrive(*cf)
    b = -first_sum(cfirst, C)
    bvec[...] = b

    def keep_b(where, v):
        Fb[where, :] = v

    spread(b, keep_b)
    first_over_rows()
    start(*rf)
    arrive(*rf)
    avec[...] = -first_sum(rfirst, R)

    def step_b(where, v):
        F[where, :] = 1.0 / v
        Fb[where, :] = Fb[where, :] - log2(v)

    @pl.loop(0, ITERS - 1)
    def _(e):
        over_cols(e, Pm)
        start(*cg(e))
        arrive(*cg(e))
        total = plain_sum(cbuf, e, C)
        bvec[...] = bvec[...] - log2(total)
        spread(total, step_b)
        over_rows(e)
        start(*rg(e))
        arrive(*rg(e))
        avec[...] = avec[...] - log2(plain_sum(rbuf, e, R))

    over_cols(ITERS - 1, Wt)
    start(*cg(ITERS - 1))

    def order(k):
        part = jnp.int32(0)
        for at, row in enumerate(ORDER):
            for step, value in enumerate(row):
                part = part + jnp.where(jnp.logical_and(z == at, k == step), value, 0)
        return part

    def weighted(part):
        return jnp.dot(Wt[...], Y[:, lanes(part, wc)], preferred_element_type=jnp.float32)

    def scaled(v):
        return jnp.concatenate([v[:, i * T:(i + 1) * T] * F[...] for i in range(wc // T)], axis=1).astype(jnp.bfloat16)

    def px_copy(k, d):
        return rdma(psend.at[k, d - 1], xrecv.at[k, d - 1], px_send.at[k, d - 1], px_recv.at[k, d - 1],
                    col=z * XN + lax.rem(x + d, XN))

    def inverse(where, v):
        F[where, :] = 1.0 / v

    head = weighted(order(0) * XN + lax.rem(x + 1, XN))
    fout[...] = (bvec[...] + nvec[...]) * UNIT
    gout[...] = (avec[...] + qvec[...]) * UNIT
    arrive(*cg(ITERS - 1))
    spread(plain_sum(cbuf, ITERS - 1, C), inverse)
    psend[0, 0] = scaled(head)
    px_copy(0, 1).start()

    @pl.loop(0, Z)
    def _(k):
        zd = order(k)
        for d in range(1, XN):
            @pl.when(jnp.logical_or(k > 0, d > 1))
            def _():
                psend[k, d - 1] = scaled(weighted(zd * XN + lax.rem(x + d, XN)))
                px_copy(k, d).start()

    @pl.loop(0, Z)
    def _(k):
        pown[k] = scaled(weighted(order(k) * XN + x))

    def x_sum(k):
        for d in range(1, XN):
            px_copy(k, d).wait_recv()
        total = pown[k].astype(jnp.float32)
        for d in range(1, XN):
            total = total + xrecv[k, d - 1].astype(jnp.float32)
        return total

    def pz_copy(k, to, slot):
        return rdma(zsend.at[k], zrecv.at[slot], pz_send.at[k], pz_recv.at[slot], col=to * XN + x)

    @pl.loop(0, Z - 1)
    def _(k):
        zd = order(k)
        right = zd > z
        more = jnp.logical_or(jnp.logical_and(right, z > 0), jnp.logical_and(zd < z, z < Z - 1))
        total = x_sum(k)

        @pl.when(more)
        def _():
            pz_copy(k, z, zd).wait_recv()
            zsend[k] = (total + zrecv[zd].astype(jnp.float32)).astype(jnp.bfloat16)

        @pl.when(jnp.logical_not(more))
        def _():
            zsend[k] = total.astype(jnp.bfloat16)

        to = jnp.where(right, z + 1, z - 1)
        slot = jnp.where(zd == z - 1, Z, zd)
        pz_copy(k, to, slot).start()

    target[...] = x_sum(Z - 1)
    for here, slot in ((z > 0, z), (z < Z - 1, Z)):
        @pl.when(here)
        def _():
            pz_copy(0, z, slot).wait_recv()
            target[...] += zrecv[slot].astype(jnp.float32)

    for cond, make in sent:
        pl.when(cond)(lambda make=make: make().wait_send())
    groups = [cf, rf] + [cg(e) for e in range(ITERS)] + [rg(e) for e in range(ITERS - 1)]
    for group in groups:
        for copy in put(*group):
            copy.wait_send()
    for k in range(Z):
        for d in range(1, XN):
            px_copy(k, d).wait_send()
    for k in range(Z - 1):
        pz_copy(k, z, 0).wait_send()


def per_device(R, C, noise_latents, data_latents, noise_sizes, data_sizes):
    rows, wc = noise_latents.shape
    cols, wr = data_latents.shape
    width = wc * C
    XN = C // Z
    f32, bf16 = jnp.float32, jnp.bfloat16
    dma = pltpu.SemaphoreType.DMA
    vmem = pl.BlockSpec(memory_space=pltpu.VMEM)
    anywhere = pl.BlockSpec(memory_space=pl.ANY)
    smem = pl.BlockSpec(memory_space=pltpu.SMEM)
    target, f, g = pl.pallas_call(
        functools.partial(kernel, R, C),
        out_shape=(
            jax.ShapeDtypeStruct((rows, wc), f32),
            jax.ShapeDtypeStruct((1, rows), f32),
            jax.ShapeDtypeStruct((1, cols), f32),
        ),
        in_specs=[anywhere, anywhere, smem, smem],
        out_specs=(vmem, vmem, vmem),
        scratch_shapes=[
            pltpu.VMEM((rows, width), bf16),
            pltpu.VMEM((cols, width), bf16),
            pltpu.VMEM((rows, cols), f32),
            pltpu.VMEM((rows, cols), f32),
            pltpu.VMEM((rows, cols), bf16),
            pltpu.VMEM((rows, T), jnp.int32),
            pltpu.VMEM((rows, T), f32),
            pltpu.VMEM((rows, T), f32),
            pltpu.VMEM((1, cols), f32),
            pltpu.VMEM((1, rows), f32),
            pltpu.VMEM((1, cols), f32),
            pltpu.VMEM((1, rows), f32),
            pltpu.VMEM((1, C, 2, rows), f32),
            pltpu.VMEM((1, R, 2, cols), f32),
            pltpu.VMEM((ITERS, C, 1, rows), f32),
            pltpu.VMEM((ITERS - 1, R, 1, cols), f32),
            pltpu.VMEM((Z, XN - 1, rows, wc), bf16),
            pltpu.VMEM((Z, rows, wc), bf16),
            pltpu.VMEM((Z, XN - 1, rows, wc), bf16),
            pltpu.VMEM((Z - 1, rows, wc), bf16),
            pltpu.VMEM((Z + 1, rows, wc), bf16),
            dma((2,)),
            dma((C, 4)),
            dma((C,)),
            dma((R, PIECES, 3)),
            dma((R, PIECES)),
            dma((1, C - 1)),
            dma((1, C)),
            dma((1, R - 1)),
            dma((1, R)),
            dma((ITERS, C - 1)),
            dma((ITERS, C)),
            dma((ITERS - 1, R - 1)),
            dma((ITERS - 1, R)),
            dma((Z, XN - 1)),
            dma((Z, XN - 1)),
            dma((Z - 1,)),
            dma((Z + 1,)),
        ],
        compiler_params=pltpu.CompilerParams(
            collective_id=0, has_side_effects=True, vmem_limit_bytes=58 * 1024 * 1024
        ),
        name="sinkhorn",
    )(noise_latents, data_latents, noise_sizes, data_sizes)
    velocity = target - noise_latents.astype(f32)
    return velocity, f.reshape(rows), g.reshape(cols)


def solution(mesh):
    placed = (P("row", "col"), P("col", "row"), P(), P())
    return jax.shard_map(
        functools.partial(per_device, mesh.shape["row"], mesh.shape["col"]),
        mesh=mesh,
        in_specs=placed,
        out_specs=(P("row", "col"), P("row"), P("col")),
        check_vma=False,
    )
```

```python
import functools
import math

import jax
import jax.numpy as jnp
from jax import lax
from jax.experimental import pallas as pl
from jax.experimental.pallas import tpu as pltpu
from jax.sharding import PartitionSpec as P

ITERS = 3
EPSILON = 0.05
MASKED = -1e30
Z = 4
CORES = 2
PIECES = 4
T = 128
UNIT = EPSILON * math.log(2.0)
ORDER = ((3, 2, 1, 0), (3, 0, 2, 1), (0, 3, 1, 2), (0, 1, 2, 3))
MESH = pl.DeviceIdType.MESH


def kernel(
    R, C, xin, yin, nsz, dsz,
    target, fout, gout,
    X, Y, S, Pm, Wt, NC, F, Fb, avec, bvec, qvec, nvec, qpart, dcvec, cfirst, rfirst, cbuf, rbuf,
    psend, pown, xrecv, zsend, zrecv,
    local_sem, xg_send, xg_recv, yg_send, yg_recv,
    cf_send, cf_recv, rf_send, rf_recv, ce_send, ce_recv, re_send, re_recv, px_send, px_recv, pz_send, pz_recv,
):
    rows, wc = xin.shape
    cols, wr = yin.shape
    width = wc * C
    XN = C // Z
    YN = R // CORES
    r = lax.axis_index("row")
    c = lax.axis_index("col")
    z, x = lax.div(c, XN), lax.rem(c, XN)
    y, core = lax.div(r, CORES), lax.rem(r, CORES)
    scale = 2.0 / (width * UNIT)

    def rdma(src, dst, send, recv, **peer):
        return pltpu.make_async_remote_copy(
            src_ref=src, dst_ref=dst, send_sem=send, recv_sem=recv,
            device_id=peer, device_id_type=MESH,
        )

    barrier = pltpu.get_barrier_semaphore()
    for k in range(1, C):
        pl.semaphore_signal(barrier, inc=1, device_id={"col": lax.rem(c + k, C)}, device_id_type=MESH)
    for k in range(1, R):
        pl.semaphore_signal(barrier, inc=1, device_id={"row": lax.rem(r + k, R)}, device_id_type=MESH)
    pl.semaphore_wait(barrier, C - 1 + R - 1)

    sent = []

    def noise_part(block):
        return X.at[:, pl.ds(pl.multiple_of(block * wc, wc), wc)]

    def noise_copy(block, way, own=False):
        peer = {0: c + XN, 1: c - XN, 2: c + 1, 3: c - 1}[way]
        return rdma(xin if own else noise_part(block), noise_part(block),
                    xg_send.at[block, way], xg_recv.at[block], col=peer)

    def can_noise(way):
        return {0: z + 1 < Z, 1: z >= 1, 2: x + 1 < XN, 3: x >= 1}[way]

    def send(cond, make):
        pl.when(cond)(lambda: make().start())
        sent.append((cond, make))

    def noise_send(block, way, cond=None, own=False):
        ok = can_noise(way) if cond is None else jnp.logical_and(cond, can_noise(way))
        send(ok, lambda: noise_copy(block, way, own))

    piece = cols // PIECES

    def data_part(block, q):
        return Y.at[pl.ds(q * piece, piece), pl.ds(pl.multiple_of(block * wr, wr), wr)]

    def data_copy(block, q, way, own=False):
        peer = {0: r + CORES, 1: r - CORES, 2: r + 1 - 2 * core}[way]
        src = yin.at[pl.ds(q * piece, piece), :] if own else data_part(block, q)
        return rdma(src, data_part(block, q), yg_send.at[block, q, way], yg_recv.at[block, q], row=peer)

    def can_data(way):
        return {0: y + 1 < YN, 1: y >= 1, 2: y >= 0}[way]

    def data_send(block, q, way, cond=None, own=False):
        ok = can_data(way) if cond is None else jnp.logical_and(cond, can_data(way))
        send(ok, lambda: data_copy(block, q, way, own))

    for way in (0, 1, 2, 3):
        noise_send(c, way, own=True)
    for q in range(PIECES):
        for way in (0, 1):
            data_send(r, q, way, own=True)
    for q in range(PIECES):
        data_send(r, q, 2, own=True)
    lx = pltpu.make_async_copy(xin, noise_part(c), local_sem.at[0])
    ly = pltpu.make_async_copy(yin, Y.at[:, pl.ds(pl.multiple_of(r * wr, wr), wr)], local_sem.at[1])
    lx.start()
    ly.start()

    def cluster(position, sizes):
        total = jnp.int32(0)
        number = jnp.zeros(position.shape, jnp.int32)
        for k in range(7):
            total = total + sizes[k]
            number = number + (position >= total).astype(jnp.int32)
        return number

    for i in range(rows // T):
        NC[pl.ds(i * T, T), :] = cluster(
            r * rows + i * T + lax.broadcasted_iota(jnp.int32, (T, T), 0), nsz)

    def take_noise(dz, dx):
        here = jnp.logical_and(
            jnp.logical_and(z + dz >= 0, z + dz < Z), jnp.logical_and(x + dx >= 0, x + dx < XN))
        block = c + dz * XN + dx
        pl.when(here)(lambda: noise_copy(block, 0).wait_recv())
        if dx == 0:
            noise_send(block, 1 if dz > 0 else 0, here)
            noise_send(block, 2, here)
            noise_send(block, 3, here)
        elif abs(dx) < XN - 1:
            noise_send(block, 3 if dx > 0 else 2, here)

    def take_data(dy, q):
        here = jnp.logical_and(y + dy >= 0, y + dy < YN)
        block = r + dy * CORES
        pl.when(here)(lambda: data_copy(block, q, 0).wait_recv())
        if abs(dy) < YN - 1:
            data_send(block, q, 1 if dy > 0 else 0, here)
        data_send(block, q, 2, here)

    def signs(d):
        return (d, -d) if d else (0,)

    sibling = r + 1 - 2 * core

    def take_sibling(dy, q):
        here = jnp.logical_and(y + dy >= 0, y + dy < YN)
        pl.when(here)(lambda: data_copy(sibling + dy * CORES, q, 0).wait_recv())

    def lanes(i, n=T):
        return pl.ds(pl.multiple_of(i * n, n), n)

    def squares(ref, i, first, wide):
        total = jnp.zeros((T, T), jnp.float32)
        for k in range(wide // T):
            v = ref[lanes(i), pl.ds(pl.multiple_of(first + k * T, T), T)].astype(jnp.float32)
            total = total + v * v
        return jnp.sum(total.T, axis=0, keepdims=True) * (1.0 / (width * UNIT))

    quarter = width // Z
    last = PIECES + 1
    early = XN == 2 and YN == 2 and R == Z

    def ready(part, q):
        if not early:
            return jnp.int32(last)
        noise_step = jnp.abs(part - z) + 1
        mine = lax.rem(part, CORES) == core
        data_step = jnp.where(lax.div(part, CORES) == y, 1, jnp.where(mine, q + 1, q + 2))
        return jnp.maximum(noise_step, data_step)

    def tasks(step):
        @pl.loop(0, Z * PIECES)
        def _(t):
            part, q = lax.div(t, PIECES), lax.rem(t, PIECES)

            @pl.when(ready(part, q) == step)
            def _():
                features = lanes(part, quarter)
                S[:, lanes(q, piece)] += lax.dot_general(
                    X[:, features], Y[lanes(q, piece), features], (((1,), (1,)), ((), ())),
                    preferred_element_type=jnp.float32)
                for h in range(piece // T):
                    i = q * (piece // T) + h
                    qpart[part, :, lanes(i)] = squares(Y, i, part * quarter, quarter)

    @pl.loop(0, rows // T)
    def _(i):
        S[lanes(i), :] = jnp.zeros((T, cols), jnp.float32)

    dcvec[...] = cluster(c * cols + lax.broadcasted_iota(jnp.int32, (1, cols), 1), dsz)

    for step in range(1, Z + 1):
        if step < Z:
            for dz in signs(step):
                take_noise(dz, 0)
        if step <= PIECES:
            for dy in signs(1):
                take_data(dy, step - 1)
        for dz in signs(step - 1):
            for dx in signs(1):
                take_noise(dz, dx)
        if step == 1:
            lx.wait()
            ly.wait()
            for q in range(PIECES):
                take_sibling(0, q)
        else:
            for dy in signs(1):
                take_sibling(dy, step - 2)
        if early:
            tasks(step)
    for step in range(2, XN):
        for dz in range(1 - Z, Z):
            for dx in signs(step):
                take_noise(dz, dx)
    for step in range(2, YN):
        for q in range(PIECES):
            for dy in signs(step):
                take_data(dy, q)
    for dy in signs(1):
        take_sibling(dy, PIECES - 1)
    for step in range(2, YN):
        for q in range(PIECES):
            for dy in signs(step):
                take_sibling(dy, q)
    tasks(last)
    total = qpart[0]
    for part in range(1, Z):
        total = total + qpart[part]
    qvec[...] = total
    avec[...] = -total

    def first_over_cols():
        @pl.loop(0, rows // T)
        def _(i):
            def term(k):
                return S[lanes(i), pl.ds(k * T, T)] + avec[:, pl.ds(k * T, T)]

            number = NC[lanes(i), :]
            top = jnp.full((T, T), MASKED, jnp.float32)
            for k in range(cols // T):
                at = pl.ds(k * T, T)
                v = jnp.where(number == dcvec[:, at], S[lanes(i), at] * scale, MASKED)
                S[lanes(i), at] = v
                top = jnp.maximum(top, v + avec[:, at])
            total = jnp.exp2(term(0) - top)
            for k in range(1, cols // T):
                total = total + jnp.exp2(term(k) - top)
            top, total = top.T, total.T
            best = jnp.max(top, axis=0, keepdims=True)
            cfirst[0, c, 0:1, lanes(i)] = best
            cfirst[0, c, 1:2, lanes(i)] = jnp.sum(total * jnp.exp2(top - best), axis=0, keepdims=True)

    def first_over_rows():
        G = 64

        @pl.loop(0, cols // T)
        def _(k):
            def term(i):
                return S[pl.ds(i * G, G), lanes(k)] + Fb[pl.ds(i * G, G), :]

            top = term(0)
            for i in range(1, rows // G):
                top = jnp.maximum(top, term(i))
            total = jnp.exp2(term(0) - top)
            for i in range(1, rows // G):
                total = total + jnp.exp2(term(i) - top)
            best = jnp.max(top, axis=0, keepdims=True)
            rfirst[0, r, 0:1, lanes(k)] = best
            rfirst[0, r, 1:2, lanes(k)] = jnp.sum(total * jnp.exp2(top - best), axis=0, keepdims=True)

    def over_cols(e, out):
        @pl.loop(0, rows // T)
        def _(i):
            b = Fb[lanes(i), :]
            total = jnp.zeros((T, T), jnp.float32)
            for k in range(cols // T):
                v = jnp.exp2(S[lanes(i), pl.ds(k * T, T)] + avec[:, pl.ds(k * T, T)] + b)
                out[lanes(i), pl.ds(k * T, T)] = v.astype(out.dtype)
                total = total + v
            cbuf[e, c, :, lanes(i)] = jnp.sum(total.T, axis=0, keepdims=True)

    def over_rows(e):
        G = 64

        @pl.loop(0, cols // T)
        def _(k):
            total = jnp.zeros((G, T), jnp.float32)
            for i in range(rows // G):
                total = total + Pm[pl.ds(i * G, G), lanes(k)] * F[pl.ds(i * G, G), :]
            rbuf[e, r, :, lanes(k)] = jnp.sum(total, axis=0, keepdims=True)

    def spread(vec, use):
        for i in range(rows // T):
            use(pl.ds(i * T, T), jnp.broadcast_to(vec[:, i * T:(i + 1) * T], (T, T)).T)

    def put(buf, send_sem, recv_sem, e, me, n, axis):
        return [
            rdma(buf.at[e, me], buf.at[e, me], send_sem.at[e, k - 1], recv_sem.at[e, me],
                 **{axis: lax.rem(me + k, n)})
            for k in range(1, n)
        ]

    def start(*group):
        for copy in put(*group):
            copy.start()

    def arrive(buf, send_sem, recv_sem, e, me, n, axis):
        for k in range(1, n):
            other = lax.rem(me + k, n)
            rdma(buf.at[e, other], buf.at[e, other], send_sem.at[e, k - 1], recv_sem.at[e, other],
                 **{axis: other}).wait_recv()

    def log2(v):
        return jnp.log(v) * (1.0 / math.log(2.0))

    def first_sum(buf, n):
        best = buf[0, 0, 0:1, :]
        for k in range(1, n):
            best = jnp.maximum(best, buf[0, k, 0:1, :])
        total = buf[0, 0, 1:2, :] * jnp.exp2(buf[0, 0, 0:1, :] - best)
        for k in range(1, n):
            total = total + buf[0, k, 1:2, :] * jnp.exp2(buf[0, k, 0:1, :] - best)
        return best + log2(total)

    def plain_sum(buf, e, n):
        total = buf[e, 0]
        for k in range(1, n):
            total = total + buf[e, k]
        return total

    cf = (cfirst, cf_send, cf_recv, 0, c, C, "col")
    rf = (rfirst, rf_send, rf_recv, 0, r, R, "row")

    def cg(e):
        return (cbuf, ce_send, ce_recv, e, c, C, "col")

    def rg(e):
        return (rbuf, re_send, re_recv, e, r, R, "row")

    first_over_cols()
    start(*cf)

    @pl.loop(0, rows // T)
    def _(i):
        nvec[:, lanes(i)] = squares(X, i, 0, width)

    arrive(*cf)
    b = -first_sum(cfirst, C)
    bvec[...] = b

    def keep_b(where, v):
        Fb[where, :] = v

    spread(b, keep_b)
    first_over_rows()
    start(*rf)
    arrive(*rf)
    avec[...] = -first_sum(rfirst, R)

    def step_b(where, v):
        F[where, :] = 1.0 / v
        Fb[where, :] = Fb[where, :] - log2(v)

    @pl.loop(0, ITERS - 1)
    def _(e):
        over_cols(e, Pm)
        start(*cg(e))
        arrive(*cg(e))
        total = plain_sum(cbuf, e, C)
        bvec[...] = bvec[...] - log2(total)
        spread(total, step_b)
        over_rows(e)
        start(*rg(e))
        arrive(*rg(e))
        avec[...] = avec[...] - log2(plain_sum(rbuf, e, R))

    over_cols(ITERS - 1, Wt)
    start(*cg(ITERS - 1))

    def order(k):
        part = jnp.int32(0)
        for at, row in enumerate(ORDER):
            for step, value in enumerate(row):
                part = part + jnp.where(jnp.logical_and(z == at, k == step), value, 0)
        return part

    def weighted(part):
        return jnp.dot(Wt[...], Y[:, lanes(part, wc)], preferred_element_type=jnp.float32)

    def scaled(v):
        return jnp.concatenate([v[:, i * T:(i + 1) * T] * F[...] for i in range(wc // T)], axis=1).astype(jnp.bfloat16)

    def px_copy(k, d):
        return rdma(psend.at[k, d - 1], xrecv.at[k, d - 1], px_send.at[k, d - 1], px_recv.at[k, d - 1],
                    col=z * XN + lax.rem(x + d, XN))

    def inverse(where, v):
        F[where, :] = 1.0 / v

    head = weighted(order(0) * XN + lax.rem(x + 1, XN))
    fout[...] = (bvec[...] + nvec[...]) * UNIT
    gout[...] = (avec[...] + qvec[...]) * UNIT
    arrive(*cg(ITERS - 1))
    spread(plain_sum(cbuf, ITERS - 1, C), inverse)
    psend[0, 0] = scaled(head)
    px_copy(0, 1).start()

    @pl.loop(0, Z)
    def _(k):
        zd = order(k)
        for d in range(1, XN):
            @pl.when(jnp.logical_or(k > 0, d > 1))
            def _():
                psend[k, d - 1] = scaled(weighted(zd * XN + lax.rem(x + d, XN)))
                px_copy(k, d).start()

    @pl.loop(0, Z)
    def _(k):
        pown[k] = scaled(weighted(order(k) * XN + x))

    def x_sum(k):
        for d in range(1, XN):
            px_copy(k, d).wait_recv()
        total = pown[k].astype(jnp.float32)
        for d in range(1, XN):
            total = total + xrecv[k, d - 1].astype(jnp.float32)
        return total

    def pz_copy(k, to, slot):
        return rdma(zsend.at[k], zrecv.at[slot], pz_send.at[k], pz_recv.at[slot], col=to * XN + x)

    @pl.loop(0, Z - 1)
    def _(k):
        zd = order(k)
        right = zd > z
        more = jnp.logical_or(jnp.logical_and(right, z > 0), jnp.logical_and(zd < z, z < Z - 1))
        total = x_sum(k)

        @pl.when(more)
        def _():
            pz_copy(k, z, zd).wait_recv()
            zsend[k] = (total + zrecv[zd].astype(jnp.float32)).astype(jnp.bfloat16)

        @pl.when(jnp.logical_not(more))
        def _():
            zsend[k] = total.astype(jnp.bfloat16)

        to = jnp.where(right, z + 1, z - 1)
        slot = jnp.where(zd == z - 1, Z, zd)
        pz_copy(k, to, slot).start()

    target[...] = x_sum(Z - 1)
    for here, slot in ((z > 0, z), (z < Z - 1, Z)):
        @pl.when(here)
        def _():
            pz_copy(0, z, slot).wait_recv()
            target[...] += zrecv[slot].astype(jnp.float32)

    for cond, make in sent:
        pl.when(cond)(lambda make=make: make().wait_send())
    groups = [cf, rf] + [cg(e) for e in range(ITERS)] + [rg(e) for e in range(ITERS - 1)]
    for group in groups:
        for copy in put(*group):
            copy.wait_send()
    for k in range(Z):
        for d in range(1, XN):
            px_copy(k, d).wait_send()
    for k in range(Z - 1):
        pz_copy(k, z, 0).wait_send()


def per_device(R, C, noise_latents, data_latents, noise_sizes, data_sizes):
    rows, wc = noise_latents.shape
    cols, wr = data_latents.shape
    width = wc * C
    XN = C // Z
    f32, bf16 = jnp.float32, jnp.bfloat16
    dma = pltpu.SemaphoreType.DMA
    vmem = pl.BlockSpec(memory_space=pltpu.VMEM)
    anywhere = pl.BlockSpec(memory_space=pl.ANY)
    smem = pl.BlockSpec(memory_space=pltpu.SMEM)
    target, f, g = pl.pallas_call(
        functools.partial(kernel, R, C),
        out_shape=(
            jax.ShapeDtypeStruct((rows, wc), f32),
            jax.ShapeDtypeStruct((1, rows), f32),
            jax.ShapeDtypeStruct((1, cols), f32),
        ),
        in_specs=[anywhere, anywhere, smem, smem],
        out_specs=(vmem, vmem, vmem),
        scratch_shapes=[
            pltpu.VMEM((rows, width), bf16),
            pltpu.VMEM((cols, width), bf16),
            pltpu.VMEM((rows, cols), f32),
            pltpu.VMEM((rows, cols), f32),
            pltpu.VMEM((rows, cols), bf16),
            pltpu.VMEM((rows, T), jnp.int32),
            pltpu.VMEM((rows, T), f32),
            pltpu.VMEM((rows, T), f32),
            pltpu.VMEM((1, cols), f32),
            pltpu.VMEM((1, rows), f32),
            pltpu.VMEM((1, cols), f32),
            pltpu.VMEM((1, rows), f32),
            pltpu.VMEM((Z, 1, cols), f32),
            pltpu.VMEM((1, cols), jnp.int32),
            pltpu.VMEM((1, C, 2, rows), f32),
            pltpu.VMEM((1, R, 2, cols), f32),
            pltpu.VMEM((ITERS, C, 1, rows), f32),
            pltpu.VMEM((ITERS - 1, R, 1, cols), f32),
            pltpu.VMEM((Z, XN - 1, rows, wc), bf16),
            pltpu.VMEM((Z, rows, wc), bf16),
            pltpu.VMEM((Z, XN - 1, rows, wc), bf16),
            pltpu.VMEM((Z - 1, rows, wc), bf16),
            pltpu.VMEM((Z + 1, rows, wc), bf16),
            dma((2,)),
            dma((C, 4)),
            dma((C,)),
            dma((R, PIECES, 3)),
            dma((R, PIECES)),
            dma((1, C - 1)),
            dma((1, C)),
            dma((1, R - 1)),
            dma((1, R)),
            dma((ITERS, C - 1)),
            dma((ITERS, C)),
            dma((ITERS - 1, R - 1)),
            dma((ITERS - 1, R)),
            dma((Z, XN - 1)),
            dma((Z, XN - 1)),
            dma((Z - 1,)),
            dma((Z + 1,)),
        ],
        compiler_params=pltpu.CompilerParams(
            collective_id=0, has_side_effects=True, vmem_limit_bytes=58 * 1024 * 1024
        ),
        name="sinkhorn",
    )(noise_latents, data_latents, noise_sizes, data_sizes)
    velocity = target - noise_latents.astype(f32)
    return velocity, f.reshape(rows), g.reshape(cols)


def solution(mesh):
    placed = (P("row", "col"), P("col", "row"), P(), P())
    return jax.shard_map(
        functools.partial(per_device, mesh.shape["row"], mesh.shape["col"]),
        mesh=mesh,
        in_specs=placed,
        out_specs=(P("row", "col"), P("row"), P("col")),
        check_vma=False,
    )
```

```python
import functools
import math

import jax
import jax.numpy as jnp
from jax import lax
from jax.experimental import pallas as pl
from jax.experimental.pallas import tpu as pltpu
from jax.sharding import PartitionSpec as P

ITERS = 3
EPSILON = 0.05
MASKED = -1e30
Z = 4
CORES = 2
PIECES = 4
T = 128
UNIT = EPSILON * math.log(2.0)
ORDER = ((3, 2, 1, 0), (3, 0, 2, 1), (0, 3, 1, 2), (0, 1, 2, 3))
MESH = pl.DeviceIdType.MESH


def kernel(
    R, C, xin, yin, nsz, dsz,
    target, fout, gout,
    X, Y, S, Pm, Wt, NC, F, Fb, avec, bvec, qvec, nvec, qpart, dcvec, cfirst, rfirst, cbuf, rbuf,
    psend, pown, xrecv, zsend, zrecv,
    local_sem, xg_send, xg_recv, xg_recv2, yg_send, yg_recv,
    cf_send, cf_recv, rf_send, rf_recv, ce_send, ce_recv, re_send, re_recv, px_send, px_recv, pz_send, pz_recv,
):
    rows, wc = xin.shape
    cols, wr = yin.shape
    width = wc * C
    XN = C // Z
    YN = R // CORES
    r = lax.axis_index("row")
    c = lax.axis_index("col")
    z, x = lax.div(c, XN), lax.rem(c, XN)
    y, core = lax.div(r, CORES), lax.rem(r, CORES)
    scale = 2.0 / (width * UNIT)

    def rdma(src, dst, send, recv, **peer):
        return pltpu.make_async_remote_copy(
            src_ref=src, dst_ref=dst, send_sem=send, recv_sem=recv,
            device_id=peer, device_id_type=MESH,
        )

    barrier = pltpu.get_barrier_semaphore()
    for k in range(1, C):
        pl.semaphore_signal(barrier, inc=1, device_id={"col": lax.rem(c + k, C)}, device_id_type=MESH)
    for k in range(1, R):
        pl.semaphore_signal(barrier, inc=1, device_id={"row": lax.rem(r + k, R)}, device_id_type=MESH)
    pl.semaphore_wait(barrier, C - 1 + R - 1)

    sent = []

    def noise_part(block):
        return X.at[:, pl.ds(pl.multiple_of(block * wc, wc), wc)]

    def noise_copy(block, way, own=False):
        peer = {0: c + XN, 1: c - XN, 2: c + 1, 3: c - 1}[way]
        return rdma(xin if own else noise_part(block), noise_part(block),
                    xg_send.at[block, way], xg_recv.at[block], col=peer)

    def can_noise(way):
        return {0: z + 1 < Z, 1: z >= 1, 2: x + 1 < XN, 3: x >= 1}[way]

    def send(cond, make):
        pl.when(cond)(lambda: make().start())
        sent.append((cond, make))

    def noise_send(block, way, cond=None, own=False):
        ok = can_noise(way) if cond is None else jnp.logical_and(cond, can_noise(way))
        send(ok, lambda: noise_copy(block, way, own))

    piece = cols // PIECES

    def data_part(block, q):
        return Y.at[pl.ds(q * piece, piece), pl.ds(pl.multiple_of(block * wr, wr), wr)]

    def data_copy(block, q, way, own=False):
        peer = {0: r + CORES, 1: r - CORES, 2: r + 1 - 2 * core}[way]
        src = yin.at[pl.ds(q * piece, piece), :] if own else data_part(block, q)
        return rdma(src, data_part(block, q), yg_send.at[block, q, way], yg_recv.at[block, q], row=peer)

    def can_data(way):
        return {0: y + 1 < YN, 1: y >= 1, 2: y >= 0}[way]

    def data_send(block, q, way, cond=None, own=False):
        ok = can_data(way) if cond is None else jnp.logical_and(cond, can_data(way))
        send(ok, lambda: data_copy(block, q, way, own))

    for way in (0, 1, 2, 3):
        noise_send(c, way, own=True)
    for q in range(PIECES):
        for way in (0, 1):
            data_send(r, q, way, own=True)
    for q in range(PIECES):
        data_send(r, q, 2, own=True)
    lx = pltpu.make_async_copy(xin, noise_part(c), local_sem.at[0])
    ly = pltpu.make_async_copy(yin, Y.at[:, pl.ds(pl.multiple_of(r * wr, wr), wr)], local_sem.at[1])
    lx.start()
    ly.start()

    def cluster(position, sizes):
        total = jnp.int32(0)
        number = jnp.zeros(position.shape, jnp.int32)
        for k in range(7):
            total = total + sizes[k]
            number = number + (position >= total).astype(jnp.int32)
        return number

    for i in range(rows // T):
        NC[pl.ds(i * T, T), :] = cluster(
            r * rows + i * T + lax.broadcasted_iota(jnp.int32, (T, T), 0), nsz)

    early = XN == 2 and YN == 2 and R == Z
    half = rows // 2

    def half_copy(block, second, way):
        peer = {0: c + XN, 1: c - XN, 2: c + 1, 3: c - 1}[way]
        part = X.at[pl.ds(half if second else 0, half), pl.ds(pl.multiple_of(block * wc, wc), wc)]
        if second:
            return rdma(part, part, xg_send.at[block, 4], xg_recv2.at[block], col=peer)
        return rdma(part, part, xg_send.at[block, way], xg_recv.at[block], col=peer)

    def is_end(dz):
        return jnp.logical_or(z + dz == 0, z + dz == Z - 1)

    def exists(dz, dx):
        return jnp.logical_and(
            jnp.logical_and(z + dz >= 0, z + dz < Z), jnp.logical_and(x + dx >= 0, x + dx < XN))

    def take_noise(dz, dx):
        here = exists(dz, dx)
        block = c + dz * XN + dx
        halves = early and abs(dz) >= 2
        if dx == 0:
            pl.when(here)(lambda: noise_copy(block, 0).wait_recv())
            noise_send(block, 1 if dz > 0 else 0, here)
            for way in (2, 3):
                if halves:
                    ok = jnp.logical_and(here, can_noise(way))
                    cut = is_end(dz)
                    send(jnp.logical_and(ok, cut), lambda way=way: half_copy(block, False, way))
                    send(jnp.logical_and(ok, jnp.logical_not(cut)), lambda way=way: noise_copy(block, way))
                else:
                    noise_send(block, way, here)
        else:
            if halves:
                here = jnp.logical_and(here, jnp.logical_not(is_end(dz)))
            pl.when(here)(lambda: noise_copy(block, 0).wait_recv())
            if abs(dx) < XN - 1:
                noise_send(block, 3 if dx > 0 else 2, here)
            if early and abs(dz) == 1:
                pass_second(block, dz, jnp.logical_and(here, is_end(dz)))

    def pass_second(block, dz, here):
        way = 1 if dz > 0 else 0
        send(jnp.logical_and(here, can_noise(way)), lambda: half_copy(block, True, way))

    def take_second(dz, dx):
        here = jnp.logical_and(exists(dz, dx), is_end(dz))
        block = c + dz * XN + dx
        pl.when(here)(lambda: half_copy(block, True, 0).wait_recv())
        if abs(dz) < Z - 1:
            pass_second(block, dz, here)

    def take_first(dz, dx):
        here = jnp.logical_and(exists(dz, dx), is_end(dz))
        block = c + dz * XN + dx
        pl.when(here)(lambda: half_copy(block, False, 0).wait_recv())

    def take_data(dy, q):
        here = jnp.logical_and(y + dy >= 0, y + dy < YN)
        block = r + dy * CORES
        pl.when(here)(lambda: data_copy(block, q, 0).wait_recv())
        if abs(dy) < YN - 1:
            data_send(block, q, 1 if dy > 0 else 0, here)
        data_send(block, q, 2, here)

    def signs(d):
        return (d, -d) if d else (0,)

    sibling = r + 1 - 2 * core

    def take_sibling(dy, q):
        here = jnp.logical_and(y + dy >= 0, y + dy < YN)
        pl.when(here)(lambda: data_copy(sibling + dy * CORES, q, 0).wait_recv())

    def lanes(i, n=T):
        return pl.ds(pl.multiple_of(i * n, n), n)

    def squares(ref, i, first, wide):
        total = jnp.zeros((T, T), jnp.float32)
        for k in range(wide // T):
            v = ref[lanes(i), pl.ds(pl.multiple_of(first + k * T, T), T)].astype(jnp.float32)
            total = total + v * v
        return jnp.sum(total.T, axis=0, keepdims=True) * (1.0 / (width * UNIT))

    quarter = width // Z
    last = PIECES + 1

    def ready(part, q):
        if not early:
            return jnp.int32(last)
        far = jnp.abs(part - z)
        cut = jnp.logical_and(far == 2, jnp.logical_or(part == 0, part == Z - 1))
        noise_step = far + 1 + cut.astype(jnp.int32)
        mine = lax.rem(part, CORES) == core
        data_step = jnp.where(lax.div(part, CORES) == y, 1, jnp.where(jnp.logical_and(mine, q < PIECES - 1), q + 1, q + 2))
        return jnp.maximum(noise_step, data_step)

    def tasks(step):
        @pl.loop(0, Z * PIECES)
        def _(t):
            part, q = lax.div(t, PIECES), lax.rem(t, PIECES)

            @pl.when(ready(part, q) == step)
            def _():
                features = lanes(part, quarter)
                S[:, lanes(q, piece)] += lax.dot_general(
                    X[:, features], Y[lanes(q, piece), features], (((1,), (1,)), ((), ())),
                    preferred_element_type=jnp.float32)
                for h in range(piece // T):
                    i = q * (piece // T) + h
                    qpart[part, :, lanes(i)] = squares(Y, i, part * quarter, quarter)

    @pl.loop(0, rows // T)
    def _(i):
        S[lanes(i), :] = jnp.zeros((T, cols), jnp.float32)

    dcvec[...] = cluster(c * cols + lax.broadcasted_iota(jnp.int32, (1, cols), 1), dsz)

    for step in range(1, Z + 1):
        if step < Z:
            for dz in signs(step):
                take_noise(dz, 0)
        if step < PIECES:
            for dy in signs(1):
                take_data(dy, step - 1)
        for dz in signs(step - 1):
            for dx in signs(1):
                if early and step == Z - 1:
                    take_second(dz, dx)
                if step < Z or not early:
                    take_noise(dz, dx)
        if early and step == Z:
            for dz in signs(Z - 1):
                for dx in signs(1):
                    take_second(dz, dx)
            for far in range(2, Z):
                for dz in signs(far):
                    for dx in signs(1):
                        take_first(dz, dx)
        if step == 1:
            lx.wait()
            ly.wait()
            for q in range(PIECES):
                take_sibling(0, q)
        else:
            for dy in signs(1):
                take_sibling(dy, step - 2)
        if early:
            tasks(step)
    for dy in signs(1):
        take_data(dy, PIECES - 1)
    for step in range(2, XN):
        for dz in range(1 - Z, Z):
            for dx in signs(step):
                take_noise(dz, dx)
    for step in range(2, YN):
        for q in range(PIECES):
            for dy in signs(step):
                take_data(dy, q)
    for dy in signs(1):
        take_sibling(dy, PIECES - 1)
    for step in range(2, YN):
        for q in range(PIECES):
            for dy in signs(step):
                take_sibling(dy, q)
    tasks(last)
    total = qpart[0]
    for part in range(1, Z):
        total = total + qpart[part]
    qvec[...] = total
    avec[...] = -total

    def first_over_cols():
        @pl.loop(0, rows // T)
        def _(i):
            def term(k):
                return S[lanes(i), pl.ds(k * T, T)] + avec[:, pl.ds(k * T, T)]

            number = NC[lanes(i), :]
            top = jnp.full((T, T), MASKED, jnp.float32)
            for k in range(cols // T):
                at = pl.ds(k * T, T)
                v = jnp.where(number == dcvec[:, at], S[lanes(i), at] * scale, MASKED)
                S[lanes(i), at] = v
                top = jnp.maximum(top, v + avec[:, at])
            total = jnp.exp2(term(0) - top)
            for k in range(1, cols // T):
                total = total + jnp.exp2(term(k) - top)
            top, total = top.T, total.T
            best = jnp.max(top, axis=0, keepdims=True)
            cfirst[0, c, 0:1, lanes(i)] = best
            cfirst[0, c, 1:2, lanes(i)] = jnp.sum(total * jnp.exp2(top - best), axis=0, keepdims=True)

    def first_over_rows():
        G = 64

        @pl.loop(0, cols // T)
        def _(k):
            def term(i):
                return S[pl.ds(i * G, G), lanes(k)] + Fb[pl.ds(i * G, G), :]

            top = term(0)
            for i in range(1, rows // G):
                top = jnp.maximum(top, term(i))
            total = jnp.exp2(term(0) - top)
            for i in range(1, rows // G):
                total = total + jnp.exp2(term(i) - top)
            best = jnp.max(top, axis=0, keepdims=True)
            rfirst[0, r, 0:1, lanes(k)] = best
            rfirst[0, r, 1:2, lanes(k)] = jnp.sum(total * jnp.exp2(top - best), axis=0, keepdims=True)

    def over_cols(e, out):
        @pl.loop(0, rows // T)
        def _(i):
            b = Fb[lanes(i), :]
            total = jnp.zeros((T, T), jnp.float32)
            for k in range(cols // T):
                v = jnp.exp2(S[lanes(i), pl.ds(k * T, T)] + avec[:, pl.ds(k * T, T)] + b)
                out[lanes(i), pl.ds(k * T, T)] = v.astype(out.dtype)
                total = total + v
            cbuf[e, c, :, lanes(i)] = jnp.sum(total.T, axis=0, keepdims=True)

    def over_rows(e):
        G = 64

        @pl.loop(0, cols // T)
        def _(k):
            total = jnp.zeros((G, T), jnp.float32)
            for i in range(rows // G):
                total = total + Pm[pl.ds(i * G, G), lanes(k)] * F[pl.ds(i * G, G), :]
            rbuf[e, r, :, lanes(k)] = jnp.sum(total, axis=0, keepdims=True)

    def spread(vec, use):
        for i in range(rows // T):
            use(pl.ds(i * T, T), jnp.broadcast_to(vec[:, i * T:(i + 1) * T], (T, T)).T)

    def put(buf, send_sem, recv_sem, e, me, n, axis):
        return [
            rdma(buf.at[e, me], buf.at[e, me], send_sem.at[e, k - 1], recv_sem.at[e, me],
                 **{axis: lax.rem(me + k, n)})
            for k in range(1, n)
        ]

    def start(*group):
        for copy in put(*group):
            copy.start()

    def arrive(buf, send_sem, recv_sem, e, me, n, axis):
        for k in range(1, n):
            other = lax.rem(me + k, n)
            rdma(buf.at[e, other], buf.at[e, other], send_sem.at[e, k - 1], recv_sem.at[e, other],
                 **{axis: other}).wait_recv()

    def log2(v):
        return jnp.log(v) * (1.0 / math.log(2.0))

    def first_sum(buf, n):
        best = buf[0, 0, 0:1, :]
        for k in range(1, n):
            best = jnp.maximum(best, buf[0, k, 0:1, :])
        total = buf[0, 0, 1:2, :] * jnp.exp2(buf[0, 0, 0:1, :] - best)
        for k in range(1, n):
            total = total + buf[0, k, 1:2, :] * jnp.exp2(buf[0, k, 0:1, :] - best)
        return best + log2(total)

    def plain_sum(buf, e, n):
        total = buf[e, 0]
        for k in range(1, n):
            total = total + buf[e, k]
        return total

    cf = (cfirst, cf_send, cf_recv, 0, c, C, "col")
    rf = (rfirst, rf_send, rf_recv, 0, r, R, "row")

    def cg(e):
        return (cbuf, ce_send, ce_recv, e, c, C, "col")

    def rg(e):
        return (rbuf, re_send, re_recv, e, r, R, "row")

    first_over_cols()
    start(*cf)

    @pl.loop(0, rows // T)
    def _(i):
        nvec[:, lanes(i)] = squares(X, i, 0, width)

    arrive(*cf)
    b = -first_sum(cfirst, C)
    bvec[...] = b

    def keep_b(where, v):
        Fb[where, :] = v

    spread(b, keep_b)
    first_over_rows()
    start(*rf)
    arrive(*rf)
    avec[...] = -first_sum(rfirst, R)

    def step_b(where, v):
        F[where, :] = 1.0 / v
        Fb[where, :] = Fb[where, :] - log2(v)

    @pl.loop(0, ITERS - 1)
    def _(e):
        over_cols(e, Pm)
        start(*cg(e))
        arrive(*cg(e))
        total = plain_sum(cbuf, e, C)
        bvec[...] = bvec[...] - log2(total)
        spread(total, step_b)
        over_rows(e)
        start(*rg(e))
        arrive(*rg(e))
        avec[...] = avec[...] - log2(plain_sum(rbuf, e, R))

    over_cols(ITERS - 1, Wt)
    start(*cg(ITERS - 1))

    def order(k):
        part = jnp.int32(0)
        for at, row in enumerate(ORDER):
            for step, value in enumerate(row):
                part = part + jnp.where(jnp.logical_and(z == at, k == step), value, 0)
        return part

    def weighted(part):
        return jnp.dot(Wt[...], Y[:, lanes(part, wc)], preferred_element_type=jnp.float32)

    def scaled(v):
        return jnp.concatenate([v[:, i * T:(i + 1) * T] * F[...] for i in range(wc // T)], axis=1).astype(jnp.bfloat16)

    def px_copy(k, d):
        return rdma(psend.at[k, d - 1], xrecv.at[k, d - 1], px_send.at[k, d - 1], px_recv.at[k, d - 1],
                    col=z * XN + lax.rem(x + d, XN))

    def inverse(where, v):
        F[where, :] = 1.0 / v

    head = weighted(order(0) * XN + lax.rem(x + 1, XN))
    fout[...] = (bvec[...] + nvec[...]) * UNIT
    gout[...] = (avec[...] + qvec[...]) * UNIT
    arrive(*cg(ITERS - 1))
    spread(plain_sum(cbuf, ITERS - 1, C), inverse)
    psend[0, 0] = scaled(head)
    px_copy(0, 1).start()

    @pl.loop(0, Z)
    def _(k):
        zd = order(k)
        for d in range(1, XN):
            @pl.when(jnp.logical_or(k > 0, d > 1))
            def _():
                psend[k, d - 1] = scaled(weighted(zd * XN + lax.rem(x + d, XN)))
                px_copy(k, d).start()

    @pl.loop(0, Z)
    def _(k):
        pown[k] = scaled(weighted(order(k) * XN + x))

    def x_sum(k):
        for d in range(1, XN):
            px_copy(k, d).wait_recv()
        total = pown[k].astype(jnp.float32)
        for d in range(1, XN):
            total = total + xrecv[k, d - 1].astype(jnp.float32)
        return total

    def pz_copy(k, to, slot):
        return rdma(zsend.at[k], zrecv.at[slot], pz_send.at[k], pz_recv.at[slot], col=to * XN + x)

    @pl.loop(0, Z - 1)
    def _(k):
        zd = order(k)
        right = zd > z
        more = jnp.logical_or(jnp.logical_and(right, z > 0), jnp.logical_and(zd < z, z < Z - 1))
        total = x_sum(k)

        @pl.when(more)
        def _():
            pz_copy(k, z, zd).wait_recv()
            zsend[k] = (total + zrecv[zd].astype(jnp.float32)).astype(jnp.bfloat16)

        @pl.when(jnp.logical_not(more))
        def _():
            zsend[k] = total.astype(jnp.bfloat16)

        to = jnp.where(right, z + 1, z - 1)
        slot = jnp.where(zd == z - 1, Z, zd)
        pz_copy(k, to, slot).start()

    target[...] = x_sum(Z - 1)
    for here, slot in ((z > 0, z), (z < Z - 1, Z)):
        @pl.when(here)
        def _():
            pz_copy(0, z, slot).wait_recv()
            target[...] += zrecv[slot].astype(jnp.float32)

    for cond, make in sent:
        pl.when(cond)(lambda make=make: make().wait_send())
    groups = [cf, rf] + [cg(e) for e in range(ITERS)] + [rg(e) for e in range(ITERS - 1)]
    for group in groups:
        for copy in put(*group):
            copy.wait_send()
    for k in range(Z):
        for d in range(1, XN):
            px_copy(k, d).wait_send()
    for k in range(Z - 1):
        pz_copy(k, z, 0).wait_send()


def per_device(R, C, noise_latents, data_latents, noise_sizes, data_sizes):
    rows, wc = noise_latents.shape
    cols, wr = data_latents.shape
    width = wc * C
    XN = C // Z
    f32, bf16 = jnp.float32, jnp.bfloat16
    dma = pltpu.SemaphoreType.DMA
    vmem = pl.BlockSpec(memory_space=pltpu.VMEM)
    anywhere = pl.BlockSpec(memory_space=pl.ANY)
    smem = pl.BlockSpec(memory_space=pltpu.SMEM)
    target, f, g = pl.pallas_call(
        functools.partial(kernel, R, C),
        out_shape=(
            jax.ShapeDtypeStruct((rows, wc), f32),
            jax.ShapeDtypeStruct((1, rows), f32),
            jax.ShapeDtypeStruct((1, cols), f32),
        ),
        in_specs=[anywhere, anywhere, smem, smem],
        out_specs=(vmem, vmem, vmem),
        scratch_shapes=[
            pltpu.VMEM((rows, width), bf16),
            pltpu.VMEM((cols, width), bf16),
            pltpu.VMEM((rows, cols), f32),
            pltpu.VMEM((rows, cols), f32),
            pltpu.VMEM((rows, cols), bf16),
            pltpu.VMEM((rows, T), jnp.int32),
            pltpu.VMEM((rows, T), f32),
            pltpu.VMEM((rows, T), f32),
            pltpu.VMEM((1, cols), f32),
            pltpu.VMEM((1, rows), f32),
            pltpu.VMEM((1, cols), f32),
            pltpu.VMEM((1, rows), f32),
            pltpu.VMEM((Z, 1, cols), f32),
            pltpu.VMEM((1, cols), jnp.int32),
            pltpu.VMEM((1, C, 2, rows), f32),
            pltpu.VMEM((1, R, 2, cols), f32),
            pltpu.VMEM((ITERS, C, 1, rows), f32),
            pltpu.VMEM((ITERS - 1, R, 1, cols), f32),
            pltpu.VMEM((Z, XN - 1, rows, wc), bf16),
            pltpu.VMEM((Z, rows, wc), bf16),
            pltpu.VMEM((Z, XN - 1, rows, wc), bf16),
            pltpu.VMEM((Z - 1, rows, wc), bf16),
            pltpu.VMEM((Z + 1, rows, wc), bf16),
            dma((2,)),
            dma((C, 5)),
            dma((C,)),
            dma((C,)),
            dma((R, PIECES, 3)),
            dma((R, PIECES)),
            dma((1, C - 1)),
            dma((1, C)),
            dma((1, R - 1)),
            dma((1, R)),
            dma((ITERS, C - 1)),
            dma((ITERS, C)),
            dma((ITERS - 1, R - 1)),
            dma((ITERS - 1, R)),
            dma((Z, XN - 1)),
            dma((Z, XN - 1)),
            dma((Z - 1,)),
            dma((Z + 1,)),
        ],
        compiler_params=pltpu.CompilerParams(
            collective_id=0, has_side_effects=True, vmem_limit_bytes=58 * 1024 * 1024
        ),
        name="sinkhorn",
    )(noise_latents, data_latents, noise_sizes, data_sizes)
    velocity = target - noise_latents.astype(f32)
    return velocity, f.reshape(rows), g.reshape(cols)


def solution(mesh):
    placed = (P("row", "col"), P("col", "row"), P(), P())
    return jax.shard_map(
        functools.partial(per_device, mesh.shape["row"], mesh.shape["col"]),
        mesh=mesh,
        in_specs=placed,
        out_specs=(P("row", "col"), P("row"), P("col")),
        check_vma=False,
    )
```

```python
import functools
import math

import jax
import jax.numpy as jnp
from jax import lax
from jax.experimental import pallas as pl
from jax.experimental.pallas import tpu as pltpu
from jax.sharding import PartitionSpec as P

ITERS = 3
EPSILON = 0.05
MASKED = -1e30
Z = 4
CORES = 2
PIECES = 4
T = 128
UNIT = EPSILON * math.log(2.0)
ORDER = ((3, 2, 1, 0), (3, 0, 2, 1), (0, 3, 1, 2), (0, 1, 2, 3))
MESH = pl.DeviceIdType.MESH


def kernel(
    R, C, xin, yin, nsz, dsz,
    target, fout, gout,
    X, Y, S, Pm, Wt, NC, F, Fb, avec, bvec, qvec, nvec, qpart, dcvec, cfirst, rfirst, cbuf, rbuf,
    psend, pown, xrecv, zsend, zrecv,
    local_sem, xg_send, xg_recv, yg_send, yg_recv,
    cf_send, cf_recv, rf_send, rf_recv, ce_send, ce_recv, re_send, re_recv, px_send, px_recv, pz_send, pz_recv,
):
    rows, wc = xin.shape
    cols, wr = yin.shape
    width = wc * C
    XN = C // Z
    YN = R // CORES
    r = lax.axis_index("row")
    c = lax.axis_index("col")
    z, x = lax.div(c, XN), lax.rem(c, XN)
    y, core = lax.div(r, CORES), lax.rem(r, CORES)
    scale = 2.0 / (width * UNIT)

    def rdma(src, dst, send, recv, **peer):
        return pltpu.make_async_remote_copy(
            src_ref=src, dst_ref=dst, send_sem=send, recv_sem=recv,
            device_id=peer, device_id_type=MESH,
        )

    barrier = pltpu.get_barrier_semaphore()
    for k in range(1, C):
        pl.semaphore_signal(barrier, inc=1, device_id={"col": lax.rem(c + k, C)}, device_id_type=MESH)
    for k in range(1, R):
        pl.semaphore_signal(barrier, inc=1, device_id={"row": lax.rem(r + k, R)}, device_id_type=MESH)
    pl.semaphore_wait(barrier, C - 1 + R - 1)

    sent = []

    def noise_part(block):
        return X.at[:, pl.ds(pl.multiple_of(block * wc, wc), wc)]

    def noise_copy(block, way, own=False):
        peer = {0: c + XN, 1: c - XN, 2: c + 1, 3: c - 1}[way]
        return rdma(xin if own else noise_part(block), noise_part(block),
                    xg_send.at[block, way], xg_recv.at[block], col=peer)

    def can_noise(way):
        return {0: z + 1 < Z, 1: z >= 1, 2: x + 1 < XN, 3: x >= 1}[way]

    def send(cond, make):
        pl.when(cond)(lambda: make().start())
        sent.append((cond, make))

    def noise_send(block, way, cond=None, own=False):
        ok = can_noise(way) if cond is None else jnp.logical_and(cond, can_noise(way))
        send(ok, lambda: noise_copy(block, way, own))

    piece = cols // PIECES

    def data_part(block, q):
        return Y.at[pl.ds(q * piece, piece), pl.ds(pl.multiple_of(block * wr, wr), wr)]

    def data_copy(block, q, way, own=False):
        peer = {0: r + CORES, 1: r - CORES, 2: r + 1 - 2 * core}[way]
        src = yin.at[pl.ds(q * piece, piece), :] if own else data_part(block, q)
        return rdma(src, data_part(block, q), yg_send.at[block, q, way], yg_recv.at[block, q], row=peer)

    def can_data(way):
        return {0: y + 1 < YN, 1: y >= 1, 2: y >= 0}[way]

    def data_send(block, q, way, cond=None, own=False):
        ok = can_data(way) if cond is None else jnp.logical_and(cond, can_data(way))
        send(ok, lambda: data_copy(block, q, way, own))

    for way in (0, 1, 2, 3):
        noise_send(c, way, own=True)
    for way in (0, 1):
        data_send(r, 0, way, own=True)
    for q in range(PIECES):
        data_send(r, q, 2, own=True)
    lx = pltpu.make_async_copy(xin, noise_part(c), local_sem.at[0])
    ly = pltpu.make_async_copy(yin, Y.at[:, pl.ds(pl.multiple_of(r * wr, wr), wr)], local_sem.at[1])
    lx.start()
    ly.start()

    def cluster(position, sizes):
        total = jnp.int32(0)
        number = jnp.zeros(position.shape, jnp.int32)
        for k in range(7):
            total = total + sizes[k]
            number = number + (position >= total).astype(jnp.int32)
        return number

    for i in range(rows // T):
        NC[pl.ds(i * T, T), :] = cluster(
            r * rows + i * T + lax.broadcasted_iota(jnp.int32, (T, T), 0), nsz)

    def take_noise(dz, dx):
        here = jnp.logical_and(
            jnp.logical_and(z + dz >= 0, z + dz < Z), jnp.logical_and(x + dx >= 0, x + dx < XN))
        block = c + dz * XN + dx
        pl.when(here)(lambda: noise_copy(block, 0).wait_recv())
        if dx == 0:
            noise_send(block, 1 if dz > 0 else 0, here)
            noise_send(block, 2, here)
            noise_send(block, 3, here)
        elif abs(dx) < XN - 1:
            noise_send(block, 3 if dx > 0 else 2, here)

    def take_data(dy, q):
        here = jnp.logical_and(y + dy >= 0, y + dy < YN)
        block = r + dy * CORES
        pl.when(here)(lambda: data_copy(block, q, 0).wait_recv())
        if abs(dy) < YN - 1:
            data_send(block, q, 1 if dy > 0 else 0, here)
        data_send(block, q, 2, here)

    def signs(d):
        return (d, -d) if d else (0,)

    sibling = r + 1 - 2 * core

    def take_sibling(dy, q):
        here = jnp.logical_and(y + dy >= 0, y + dy < YN)
        pl.when(here)(lambda: data_copy(sibling + dy * CORES, q, 0).wait_recv())

    def lanes(i, n=T):
        return pl.ds(pl.multiple_of(i * n, n), n)

    def squares(ref, i, first, wide):
        total = jnp.zeros((T, T), jnp.float32)
        for k in range(wide // T):
            v = ref[lanes(i), pl.ds(pl.multiple_of(first + k * T, T), T)].astype(jnp.float32)
            total = total + v * v
        return jnp.sum(total.T, axis=0, keepdims=True) * (1.0 / (width * UNIT))

    quarter = width // Z
    last = PIECES + 1
    early = XN == 2 and YN == 2 and R == Z

    def ready(part, q):
        if not early:
            return jnp.int32(last)
        noise_step = jnp.abs(part - z) + 1
        mine = lax.rem(part, CORES) == core
        data_step = jnp.where(lax.div(part, CORES) == y, 1, jnp.where(mine, q + 1, q + 2))
        return jnp.maximum(noise_step, data_step)

    def tasks(step):
        @pl.loop(0, Z * PIECES)
        def _(t):
            part, q = lax.div(t, PIECES), lax.rem(t, PIECES)

            @pl.when(ready(part, q) == step)
            def _():
                features = lanes(part, quarter)
                S[:, lanes(q, piece)] += lax.dot_general(
                    X[:, features], Y[lanes(q, piece), features], (((1,), (1,)), ((), ())),
                    preferred_element_type=jnp.float32)
                for h in range(piece // T):
                    i = q * (piece // T) + h
                    qpart[part, :, lanes(i)] = squares(Y, i, part * quarter, quarter)

    @pl.loop(0, rows // T)
    def _(i):
        S[lanes(i), :] = jnp.zeros((T, cols), jnp.float32)

    dcvec[...] = cluster(c * cols + lax.broadcasted_iota(jnp.int32, (1, cols), 1), dsz)

    for step in range(1, Z + 1):
        if step < Z:
            for dz in signs(step):
                take_noise(dz, 0)
        if step <= PIECES:
            for dy in signs(1):
                take_data(dy, step - 1)
            if step < PIECES:
                for way in (0, 1):
                    data_send(r, step, way, own=True)
        for dz in signs(step - 1):
            for dx in signs(1):
                take_noise(dz, dx)
        if step == 1:
            lx.wait()
            ly.wait()
            for q in range(PIECES):
                take_sibling(0, q)
        else:
            for dy in signs(1):
                take_sibling(dy, step - 2)
        if early:
            tasks(step)
    for step in range(2, XN):
        for dz in range(1 - Z, Z):
            for dx in signs(step):
                take_noise(dz, dx)
    for step in range(2, YN):
        for q in range(PIECES):
            for dy in signs(step):
                take_data(dy, q)
    for dy in signs(1):
        take_sibling(dy, PIECES - 1)
    for step in range(2, YN):
        for q in range(PIECES):
            for dy in signs(step):
                take_sibling(dy, q)
    tasks(last)
    total = qpart[0]
    for part in range(1, Z):
        total = total + qpart[part]
    qvec[...] = total
    avec[...] = -total

    def first_over_cols():
        @pl.loop(0, rows // T)
        def _(i):
            def term(k):
                return S[lanes(i), pl.ds(k * T, T)] + avec[:, pl.ds(k * T, T)]

            number = NC[lanes(i), :]
            top = jnp.full((T, T), MASKED, jnp.float32)
            for k in range(cols // T):
                at = pl.ds(k * T, T)
                v = jnp.where(number == dcvec[:, at], S[lanes(i), at] * scale, MASKED)
                S[lanes(i), at] = v
                top = jnp.maximum(top, v + avec[:, at])
            total = jnp.exp2(term(0) - top)
            for k in range(1, cols // T):
                total = total + jnp.exp2(term(k) - top)
            top, total = top.T, total.T
            best = jnp.max(top, axis=0, keepdims=True)
            cfirst[0, c, 0:1, lanes(i)] = best
            cfirst[0, c, 1:2, lanes(i)] = jnp.sum(total * jnp.exp2(top - best), axis=0, keepdims=True)

    def first_over_rows():
        G = 64

        @pl.loop(0, cols // T)
        def _(k):
            def term(i):
                return S[pl.ds(i * G, G), lanes(k)] + Fb[pl.ds(i * G, G), :]

            top = term(0)
            for i in range(1, rows // G):
                top = jnp.maximum(top, term(i))
            total = jnp.exp2(term(0) - top)
            for i in range(1, rows // G):
                total = total + jnp.exp2(term(i) - top)
            best = jnp.max(top, axis=0, keepdims=True)
            rfirst[0, r, 0:1, lanes(k)] = best
            rfirst[0, r, 1:2, lanes(k)] = jnp.sum(total * jnp.exp2(top - best), axis=0, keepdims=True)

    def over_cols(e, out):
        @pl.loop(0, rows // T)
        def _(i):
            b = Fb[lanes(i), :]
            total = jnp.zeros((T, T), jnp.float32)
            for k in range(cols // T):
                v = jnp.exp2(S[lanes(i), pl.ds(k * T, T)] + avec[:, pl.ds(k * T, T)] + b)
                out[lanes(i), pl.ds(k * T, T)] = v.astype(out.dtype)
                total = total + v
            cbuf[e, c, :, lanes(i)] = jnp.sum(total.T, axis=0, keepdims=True)

    def over_rows(e):
        G = 64

        @pl.loop(0, cols // T)
        def _(k):
            total = jnp.zeros((G, T), jnp.float32)
            for i in range(rows // G):
                total = total + Pm[pl.ds(i * G, G), lanes(k)] * F[pl.ds(i * G, G), :]
            rbuf[e, r, :, lanes(k)] = jnp.sum(total, axis=0, keepdims=True)

    def spread(vec, use):
        for i in range(rows // T):
            use(pl.ds(i * T, T), jnp.broadcast_to(vec[:, i * T:(i + 1) * T], (T, T)).T)

    def put(buf, send_sem, recv_sem, e, me, n, axis):
        return [
            rdma(buf.at[e, me], buf.at[e, me], send_sem.at[e, k - 1], recv_sem.at[e, me],
                 **{axis: lax.rem(me + k, n)})
            for k in range(1, n)
        ]

    def start(*group):
        for copy in put(*group):
            copy.start()

    def arrive(buf, send_sem, recv_sem, e, me, n, axis):
        for k in range(1, n):
            other = lax.rem(me + k, n)
            rdma(buf.at[e, other], buf.at[e, other], send_sem.at[e, k - 1], recv_sem.at[e, other],
                 **{axis: other}).wait_recv()

    def log2(v):
        return jnp.log(v) * (1.0 / math.log(2.0))

    def first_sum(buf, n):
        best = buf[0, 0, 0:1, :]
        for k in range(1, n):
            best = jnp.maximum(best, buf[0, k, 0:1, :])
        total = buf[0, 0, 1:2, :] * jnp.exp2(buf[0, 0, 0:1, :] - best)
        for k in range(1, n):
            total = total + buf[0, k, 1:2, :] * jnp.exp2(buf[0, k, 0:1, :] - best)
        return best + log2(total)

    def plain_sum(buf, e, n):
        total = buf[e, 0]
        for k in range(1, n):
            total = total + buf[e, k]
        return total

    cf = (cfirst, cf_send, cf_recv, 0, c, C, "col")
    rf = (rfirst, rf_send, rf_recv, 0, r, R, "row")

    def cg(e):
        return (cbuf, ce_send, ce_recv, e, c, C, "col")

    def rg(e):
        return (rbuf, re_send, re_recv, e, r, R, "row")

    first_over_cols()
    start(*cf)

    @pl.loop(0, rows // T)
    def _(i):
        nvec[:, lanes(i)] = squares(X, i, 0, width)

    arrive(*cf)
    b = -first_sum(cfirst, C)
    bvec[...] = b

    def keep_b(where, v):
        Fb[where, :] = v

    spread(b, keep_b)
    first_over_rows()
    start(*rf)
    arrive(*rf)
    avec[...] = -first_sum(rfirst, R)

    def step_b(where, v):
        F[where, :] = 1.0 / v
        Fb[where, :] = Fb[where, :] - log2(v)

    @pl.loop(0, ITERS - 1)
    def _(e):
        over_cols(e, Pm)
        start(*cg(e))
        arrive(*cg(e))
        total = plain_sum(cbuf, e, C)
        bvec[...] = bvec[...] - log2(total)
        spread(total, step_b)
        over_rows(e)
        start(*rg(e))
        arrive(*rg(e))
        avec[...] = avec[...] - log2(plain_sum(rbuf, e, R))

    over_cols(ITERS - 1, Wt)
    start(*cg(ITERS - 1))

    def order(k):
        part = jnp.int32(0)
        for at, row in enumerate(ORDER):
            for step, value in enumerate(row):
                part = part + jnp.where(jnp.logical_and(z == at, k == step), value, 0)
        return part

    def weighted(part):
        return jnp.dot(Wt[...], Y[:, lanes(part, wc)], preferred_element_type=jnp.float32)

    def scaled(v):
        return jnp.concatenate([v[:, i * T:(i + 1) * T] * F[...] for i in range(wc // T)], axis=1).astype(jnp.bfloat16)

    def px_copy(k, d):
        return rdma(psend.at[k, d - 1], xrecv.at[k, d - 1], px_send.at[k, d - 1], px_recv.at[k, d - 1],
                    col=z * XN + lax.rem(x + d, XN))

    def inverse(where, v):
        F[where, :] = 1.0 / v

    head = weighted(order(0) * XN + lax.rem(x + 1, XN))
    fout[...] = (bvec[...] + nvec[...]) * UNIT
    gout[...] = (avec[...] + qvec[...]) * UNIT
    arrive(*cg(ITERS - 1))
    spread(plain_sum(cbuf, ITERS - 1, C), inverse)
    psend[0, 0] = scaled(head)
    px_copy(0, 1).start()

    @pl.loop(0, Z)
    def _(k):
        zd = order(k)
        for d in range(1, XN):
            @pl.when(jnp.logical_or(k > 0, d > 1))
            def _():
                psend[k, d - 1] = scaled(weighted(zd * XN + lax.rem(x + d, XN)))

                @pl.when(k == 0)
                def _():
                    px_copy(k, d).start()

    @pl.loop(0, Z)
    def _(k):
        pown[k] = scaled(weighted(order(k) * XN + x))

    def x_sum(k):
        for d in range(1, XN):
            px_copy(k, d).wait_recv()
        total = pown[k].astype(jnp.float32)
        for d in range(1, XN):
            total = total + xrecv[k, d - 1].astype(jnp.float32)
        return total

    def pz_copy(k, to, slot):
        return rdma(zsend.at[k], zrecv.at[slot], pz_send.at[k], pz_recv.at[slot], col=to * XN + x)

    @pl.loop(0, Z - 1)
    def _(k):
        zd = order(k)
        right = zd > z
        more = jnp.logical_or(jnp.logical_and(right, z > 0), jnp.logical_and(zd < z, z < Z - 1))
        total = x_sum(k)
        for d in range(1, XN):
            px_copy(k + 1, d).start()

        @pl.when(more)
        def _():
            pz_copy(k, z, zd).wait_recv()
            zsend[k] = (total + zrecv[zd].astype(jnp.float32)).astype(jnp.bfloat16)

        @pl.when(jnp.logical_not(more))
        def _():
            zsend[k] = total.astype(jnp.bfloat16)

        to = jnp.where(right, z + 1, z - 1)
        slot = jnp.where(zd == z - 1, Z, zd)
        pz_copy(k, to, slot).start()

    target[...] = x_sum(Z - 1)
    for here, slot in ((z > 0, z), (z < Z - 1, Z)):
        @pl.when(here)
        def _():
            pz_copy(0, z, slot).wait_recv()
            target[...] += zrecv[slot].astype(jnp.float32)

    for cond, make in sent:
        pl.when(cond)(lambda make=make: make().wait_send())
    groups = [cf, rf] + [cg(e) for e in range(ITERS)] + [rg(e) for e in range(ITERS - 1)]
    for group in groups:
        for copy in put(*group):
            copy.wait_send()
    for k in range(Z):
        for d in range(1, XN):
            px_copy(k, d).wait_send()
    for k in range(Z - 1):
        pz_copy(k, z, 0).wait_send()


def per_device(R, C, noise_latents, data_latents, noise_sizes, data_sizes):
    rows, wc = noise_latents.shape
    cols, wr = data_latents.shape
    width = wc * C
    XN = C // Z
    f32, bf16 = jnp.float32, jnp.bfloat16
    dma = pltpu.SemaphoreType.DMA
    vmem = pl.BlockSpec(memory_space=pltpu.VMEM)
    anywhere = pl.BlockSpec(memory_space=pl.ANY)
    smem = pl.BlockSpec(memory_space=pltpu.SMEM)
    target, f, g = pl.pallas_call(
        functools.partial(kernel, R, C),
        out_shape=(
            jax.ShapeDtypeStruct((rows, wc), f32),
            jax.ShapeDtypeStruct((1, rows), f32),
            jax.ShapeDtypeStruct((1, cols), f32),
        ),
        in_specs=[anywhere, anywhere, smem, smem],
        out_specs=(vmem, vmem, vmem),
        scratch_shapes=[
            pltpu.VMEM((rows, width), bf16),
            pltpu.VMEM((cols, width), bf16),
            pltpu.VMEM((rows, cols), f32),
            pltpu.VMEM((rows, cols), f32),
            pltpu.VMEM((rows, cols), bf16),
            pltpu.VMEM((rows, T), jnp.int32),
            pltpu.VMEM((rows, T), f32),
            pltpu.VMEM((rows, T), f32),
            pltpu.VMEM((1, cols), f32),
            pltpu.VMEM((1, rows), f32),
            pltpu.VMEM((1, cols), f32),
            pltpu.VMEM((1, rows), f32),
            pltpu.VMEM((Z, 1, cols), f32),
            pltpu.VMEM((1, cols), jnp.int32),
            pltpu.VMEM((1, C, 2, rows), f32),
            pltpu.VMEM((1, R, 2, cols), f32),
            pltpu.VMEM((ITERS, C, 1, rows), f32),
            pltpu.VMEM((ITERS - 1, R, 1, cols), f32),
            pltpu.VMEM((Z, XN - 1, rows, wc), bf16),
            pltpu.VMEM((Z, rows, wc), bf16),
            pltpu.VMEM((Z, XN - 1, rows, wc), bf16),
            pltpu.VMEM((Z - 1, rows, wc), bf16),
            pltpu.VMEM((Z + 1, rows, wc), bf16),
            dma((2,)),
            dma((C, 4)),
            dma((C,)),
            dma((R, PIECES, 3)),
            dma((R, PIECES)),
            dma((1, C - 1)),
            dma((1, C)),
            dma((1, R - 1)),
            dma((1, R)),
            dma((ITERS, C - 1)),
            dma((ITERS, C)),
            dma((ITERS - 1, R - 1)),
            dma((ITERS - 1, R)),
            dma((Z, XN - 1)),
            dma((Z, XN - 1)),
            dma((Z - 1,)),
            dma((Z + 1,)),
        ],
        compiler_params=pltpu.CompilerParams(
            collective_id=0, has_side_effects=True, vmem_limit_bytes=58 * 1024 * 1024
        ),
        name="sinkhorn",
    )(noise_latents, data_latents, noise_sizes, data_sizes)
    velocity = target - noise_latents.astype(f32)
    return velocity, f.reshape(rows), g.reshape(cols)


def solution(mesh):
    placed = (P("row", "col"), P("col", "row"), P(), P())
    return jax.shard_map(
        functools.partial(per_device, mesh.shape["row"], mesh.shape["col"]),
        mesh=mesh,
        in_specs=placed,
        out_specs=(P("row", "col"), P("row"), P("col")),
        check_vma=False,
    )
```

```python
import functools
import math

import jax
import jax.numpy as jnp
from jax import lax
from jax.experimental import pallas as pl
from jax.experimental.pallas import tpu as pltpu
from jax.sharding import PartitionSpec as P

ITERS = 3
EPSILON = 0.05
MASKED = -1e30
Z = 4
CORES = 2
PIECES = 4
T = 128
UNIT = EPSILON * math.log(2.0)
ORDER = ((3, 2, 1, 0), (3, 0, 2, 1), (0, 3, 1, 2), (0, 1, 2, 3))
MESH = pl.DeviceIdType.MESH


def kernel(
    R, C, xin, yin, nsz, dsz,
    target, fout, gout,
    X, Y, S, Pm, Wt, NC, F, Fb, avec, bvec, qvec, nvec, qpart, dcvec, cfirst, rfirst, cbuf, rbuf,
    psend, pown, xrecv, zsend, zrecv,
    local_sem, xg_send, xg_recv, yg_send, yg_recv,
    cf_send, cf_recv, rf_send, rf_recv, ce_send, ce_recv, re_send, re_recv, px_send, px_recv, pz_send, pz_recv,
):
    rows, wc = xin.shape
    cols, wr = yin.shape
    width = wc * C
    XN = C // Z
    YN = R // CORES
    r = lax.axis_index("row")
    c = lax.axis_index("col")
    z, x = lax.div(c, XN), lax.rem(c, XN)
    y, core = lax.div(r, CORES), lax.rem(r, CORES)
    scale = 2.0 / (width * UNIT)

    def rdma(src, dst, send, recv, **peer):
        return pltpu.make_async_remote_copy(
            src_ref=src, dst_ref=dst, send_sem=send, recv_sem=recv,
            device_id=peer, device_id_type=MESH,
        )

    barrier = pltpu.get_barrier_semaphore()
    for k in range(1, C):
        pl.semaphore_signal(barrier, inc=1, device_id={"col": lax.rem(c + k, C)}, device_id_type=MESH)
    for k in range(1, R):
        pl.semaphore_signal(barrier, inc=1, device_id={"row": lax.rem(r + k, R)}, device_id_type=MESH)
    pl.semaphore_wait(barrier, C - 1 + R - 1)

    sent = []

    def noise_part(block):
        return X.at[:, pl.ds(pl.multiple_of(block * wc, wc), wc)]

    def noise_copy(block, way, own=False):
        peer = {0: c + XN, 1: c - XN, 2: c + 1, 3: c - 1}[way]
        return rdma(xin if own else noise_part(block), noise_part(block),
                    xg_send.at[block, way], xg_recv.at[block], col=peer)

    def can_noise(way):
        return {0: z + 1 < Z, 1: z >= 1, 2: x + 1 < XN, 3: x >= 1}[way]

    def send(cond, make):
        pl.when(cond)(lambda: make().start())
        sent.append((cond, make))

    def noise_send(block, way, cond=None, own=False):
        ok = can_noise(way) if cond is None else jnp.logical_and(cond, can_noise(way))
        send(ok, lambda: noise_copy(block, way, own))

    piece = cols // PIECES

    def data_part(block, q):
        return Y.at[pl.ds(q * piece, piece), pl.ds(pl.multiple_of(block * wr, wr), wr)]

    def data_copy(block, q, way, own=False):
        peer = {0: r + CORES, 1: r - CORES, 2: r + 1 - 2 * core}[way]
        src = yin.at[pl.ds(q * piece, piece), :] if own else data_part(block, q)
        return rdma(src, data_part(block, q), yg_send.at[block, q, way], yg_recv.at[block, q], row=peer)

    def can_data(way):
        return {0: y + 1 < YN, 1: y >= 1, 2: y >= 0}[way]

    def data_send(block, q, way, cond=None, own=False):
        ok = can_data(way) if cond is None else jnp.logical_and(cond, can_data(way))
        send(ok, lambda: data_copy(block, q, way, own))

    for way in (0, 1, 2, 3):
        noise_send(c, way, own=True)
    for q in range(PIECES):
        for way in (0, 1):
            data_send(r, q, way, own=True)
    for q in range(PIECES):
        data_send(r, q, 2, own=True)
    lx = pltpu.make_async_copy(xin, noise_part(c), local_sem.at[0])
    ly = pltpu.make_async_copy(yin, Y.at[:, pl.ds(pl.multiple_of(r * wr, wr), wr)], local_sem.at[1])
    lx.start()
    ly.start()

    def cluster(position, sizes):
        total = jnp.int32(0)
        number = jnp.zeros(position.shape, jnp.int32)
        for k in range(7):
            total = total + sizes[k]
            number = number + (position >= total).astype(jnp.int32)
        return number

    for i in range(rows // T):
        NC[pl.ds(i * T, T), :] = cluster(
            r * rows + i * T + lax.broadcasted_iota(jnp.int32, (T, T), 0), nsz)

    def take_noise(dz, dx):
        here = jnp.logical_and(
            jnp.logical_and(z + dz >= 0, z + dz < Z), jnp.logical_and(x + dx >= 0, x + dx < XN))
        block = c + dz * XN + dx
        pl.when(here)(lambda: noise_copy(block, 0).wait_recv())
        if dx == 0:
            noise_send(block, 1 if dz > 0 else 0, here)
            noise_send(block, 2, here)
            noise_send(block, 3, here)
        elif abs(dx) < XN - 1:
            noise_send(block, 3 if dx > 0 else 2, here)

    def take_data(dy, q):
        here = jnp.logical_and(y + dy >= 0, y + dy < YN)
        block = r + dy * CORES
        pl.when(here)(lambda: data_copy(block, q, 0).wait_recv())
        if abs(dy) < YN - 1:
            data_send(block, q, 1 if dy > 0 else 0, here)
        data_send(block, q, 2, here)

    def signs(d):
        return (d, -d) if d else (0,)

    sibling = r + 1 - 2 * core

    def take_sibling(dy, q):
        here = jnp.logical_and(y + dy >= 0, y + dy < YN)
        pl.when(here)(lambda: data_copy(sibling + dy * CORES, q, 0).wait_recv())

    def lanes(i, n=T):
        return pl.ds(pl.multiple_of(i * n, n), n)

    def squares(ref, i, first, wide):
        total = jnp.zeros((T, T), jnp.float32)
        for k in range(wide // T):
            v = ref[lanes(i), pl.ds(pl.multiple_of(first + k * T, T), T)].astype(jnp.float32)
            total = total + v * v
        return jnp.sum(total.T, axis=0, keepdims=True) * (1.0 / (width * UNIT))

    quarter = width // Z
    last = PIECES + 1
    early = XN == 2 and YN == 2 and R == Z

    def ready(part, q):
        if not early:
            return jnp.int32(last)
        noise_step = jnp.abs(part - z) + 1
        mine = lax.rem(part, CORES) == core
        data_step = jnp.where(lax.div(part, CORES) == y, 1, jnp.where(mine, q + 1, q + 2))
        return jnp.maximum(noise_step, data_step)

    def tasks(step):
        @pl.loop(0, Z * PIECES)
        def _(t):
            part, q = lax.div(t, PIECES), lax.rem(t, PIECES)

            @pl.when(ready(part, q) == step)
            def _():
                features = lanes(part, quarter)
                S[:, lanes(q, piece)] += lax.dot_general(
                    X[:, features], Y[lanes(q, piece), features], (((1,), (1,)), ((), ())),
                    preferred_element_type=jnp.float32)
                for h in range(piece // T):
                    i = q * (piece // T) + h
                    qpart[part, :, lanes(i)] = squares(Y, i, part * quarter, quarter)

    @pl.loop(0, rows // T)
    def _(i):
        S[lanes(i), :] = jnp.zeros((T, cols), jnp.float32)

    dcvec[...] = cluster(c * cols + lax.broadcasted_iota(jnp.int32, (1, cols), 1), dsz)

    for step in range(1, Z + 1):
        if step < Z:
            for dz in signs(step):
                take_noise(dz, 0)
        if step <= PIECES:
            for dy in signs(1):
                take_data(dy, step - 1)
        for dz in signs(step - 1):
            for dx in signs(1):
                take_noise(dz, dx)
        if step == 1:
            lx.wait()
            ly.wait()
            for q in range(PIECES):
                take_sibling(0, q)
        else:
            for dy in signs(1):
                take_sibling(dy, step - 2)
        if early:
            tasks(step)
    for step in range(2, XN):
        for dz in range(1 - Z, Z):
            for dx in signs(step):
                take_noise(dz, dx)
    for step in range(2, YN):
        for q in range(PIECES):
            for dy in signs(step):
                take_data(dy, q)
    for dy in signs(1):
        take_sibling(dy, PIECES - 1)
    for step in range(2, YN):
        for q in range(PIECES):
            for dy in signs(step):
                take_sibling(dy, q)
    tasks(last)
    total = qpart[0]
    for part in range(1, Z):
        total = total + qpart[part]
    qvec[...] = total
    avec[...] = -total

    def first_over_cols():
        @pl.loop(0, rows // T)
        def _(i):
            def term(k):
                return S[lanes(i), pl.ds(k * T, T)] + avec[:, pl.ds(k * T, T)]

            number = NC[lanes(i), :]
            top = jnp.full((T, T), MASKED, jnp.float32)
            for k in range(cols // T):
                at = pl.ds(k * T, T)
                v = jnp.where(number == dcvec[:, at], S[lanes(i), at] * scale, MASKED)
                S[lanes(i), at] = v
                top = jnp.maximum(top, v + avec[:, at])
            total = jnp.exp2(term(0) - top)
            for k in range(1, cols // T):
                total = total + jnp.exp2(term(k) - top)
            top, total = top.T, total.T
            best = jnp.max(top, axis=0, keepdims=True)
            cfirst[0, c, 0:1, lanes(i)] = best
            cfirst[0, c, 1:2, lanes(i)] = jnp.sum(total * jnp.exp2(top - best), axis=0, keepdims=True)

    def first_over_rows():
        G = 64

        @pl.loop(0, cols // T)
        def _(k):
            def term(i):
                return S[pl.ds(i * G, G), lanes(k)] + Fb[pl.ds(i * G, G), :]

            top = term(0)
            for i in range(1, rows // G):
                top = jnp.maximum(top, term(i))
            total = jnp.exp2(term(0) - top)
            for i in range(1, rows // G):
                total = total + jnp.exp2(term(i) - top)
            best = jnp.max(top, axis=0, keepdims=True)
            rfirst[0, r, 0:1, lanes(k)] = best
            rfirst[0, r, 1:2, lanes(k)] = jnp.sum(total * jnp.exp2(top - best), axis=0, keepdims=True)

    def over_cols(e, out):
        @pl.loop(0, rows // T)
        def _(i):
            b = Fb[lanes(i), :]
            total = jnp.zeros((T, T), jnp.float32)
            for k in range(cols // T):
                v = jnp.exp2(S[lanes(i), pl.ds(k * T, T)] + avec[:, pl.ds(k * T, T)] + b)
                out[lanes(i), pl.ds(k * T, T)] = v.astype(out.dtype)
                total = total + v
            cbuf[e, c, :, lanes(i)] = jnp.sum(total.T, axis=0, keepdims=True)

    def over_rows(e):
        G = 64

        @pl.loop(0, cols // T)
        def _(k):
            total = jnp.zeros((G, T), jnp.float32)
            for i in range(rows // G):
                total = total + Pm[pl.ds(i * G, G), lanes(k)] * F[pl.ds(i * G, G), :]
            rbuf[e, r, :, lanes(k)] = jnp.sum(total, axis=0, keepdims=True)

    def spread(vec, use):
        for i in range(rows // T):
            use(pl.ds(i * T, T), jnp.broadcast_to(vec[:, i * T:(i + 1) * T], (T, T)).T)

    def put(buf, send_sem, recv_sem, e, me, n, axis):
        return [
            rdma(buf.at[e, me], buf.at[e, me], send_sem.at[e, k - 1], recv_sem.at[e, me],
                 **{axis: lax.rem(me + k, n)})
            for k in range(1, n)
        ]

    def start(*group):
        for copy in put(*group):
            copy.start()

    def arrive(buf, send_sem, recv_sem, e, me, n, axis):
        for k in range(1, n):
            other = lax.rem(me + k, n)
            rdma(buf.at[e, other], buf.at[e, other], send_sem.at[e, k - 1], recv_sem.at[e, other],
                 **{axis: other}).wait_recv()

    def log2(v):
        return jnp.log(v) * (1.0 / math.log(2.0))

    def first_sum(buf, n):
        best = buf[0, 0, 0:1, :]
        for k in range(1, n):
            best = jnp.maximum(best, buf[0, k, 0:1, :])
        total = buf[0, 0, 1:2, :] * jnp.exp2(buf[0, 0, 0:1, :] - best)
        for k in range(1, n):
            total = total + buf[0, k, 1:2, :] * jnp.exp2(buf[0, k, 0:1, :] - best)
        return best + log2(total)

    def plain_sum(buf, e, n):
        total = buf[e, 0]
        for k in range(1, n):
            total = total + buf[e, k]
        return total

    cf = (cfirst, cf_send, cf_recv, 0, c, C, "col")
    rf = (rfirst, rf_send, rf_recv, 0, r, R, "row")

    def cg(e):
        return (cbuf, ce_send, ce_recv, e, c, C, "col")

    def rg(e):
        return (rbuf, re_send, re_recv, e, r, R, "row")

    first_over_cols()
    start(*cf)

    @pl.loop(0, rows // T)
    def _(i):
        nvec[:, lanes(i)] = squares(X, i, 0, width)

    arrive(*cf)
    b = -first_sum(cfirst, C)
    bvec[...] = b

    def keep_b(where, v):
        Fb[where, :] = v

    spread(b, keep_b)
    first_over_rows()
    start(*rf)
    arrive(*rf)
    avec[...] = -first_sum(rfirst, R)

    def step_b(where, v):
        F[where, :] = 1.0 / v
        Fb[where, :] = Fb[where, :] - log2(v)

    @pl.loop(0, ITERS - 1)
    def _(e):
        over_cols(e, Pm)
        start(*cg(e))
        arrive(*cg(e))
        total = plain_sum(cbuf, e, C)
        bvec[...] = bvec[...] - log2(total)
        spread(total, step_b)
        over_rows(e)
        start(*rg(e))
        arrive(*rg(e))
        avec[...] = avec[...] - log2(plain_sum(rbuf, e, R))

    over_cols(ITERS - 1, Wt)
    start(*cg(ITERS - 1))

    def order(k):
        part = jnp.int32(0)
        for at, row in enumerate(ORDER):
            for step, value in enumerate(row):
                part = part + jnp.where(jnp.logical_and(z == at, k == step), value, 0)
        return part

    half = rows // 2

    def weighted(part, h):
        return jnp.dot(Wt[lanes(h, half), :], Y[:, lanes(part, wc)], preferred_element_type=jnp.float32)

    def scaled(v, h):
        by = F[lanes(h, half), :]
        return jnp.concatenate([v[:, i * T:(i + 1) * T] * by for i in range(wc // T)], axis=1).astype(jnp.bfloat16)

    def px_copy(k, d, h):
        return rdma(psend.at[k, d - 1, h], xrecv.at[k, d - 1, h], px_send.at[k, d - 1, h], px_recv.at[k, d - 1, h],
                    col=z * XN + lax.rem(x + d, XN))

    def inverse(where, v):
        F[where, :] = 1.0 / v

    head = weighted(order(0) * XN + lax.rem(x + 1, XN), 0)
    fout[...] = (bvec[...] + nvec[...]) * UNIT
    gout[...] = (avec[...] + qvec[...]) * UNIT
    arrive(*cg(ITERS - 1))
    spread(plain_sum(cbuf, ITERS - 1, C), inverse)
    psend[0, 0, 0] = scaled(head, 0)
    px_copy(0, 1, 0).start()

    @pl.loop(0, Z * 2)
    def _(n):
        k, h = lax.div(n, 2), lax.rem(n, 2)
        zd = order(k)
        for d in range(1, XN):
            @pl.when(jnp.logical_or(n > 0, d > 1))
            def _():
                psend[k, d - 1, h] = scaled(weighted(zd * XN + lax.rem(x + d, XN), h), h)
                px_copy(k, d, h).start()

    @pl.loop(0, Z * 2)
    def _(n):
        k, h = lax.div(n, 2), lax.rem(n, 2)
        pown[k, h] = scaled(weighted(order(k) * XN + x, h), h)

    def x_sum(k, h):
        for d in range(1, XN):
            px_copy(k, d, h).wait_recv()
        total = pown[k, h].astype(jnp.float32)
        for d in range(1, XN):
            total = total + xrecv[k, d - 1, h].astype(jnp.float32)
        return total

    def pz_copy(k, to, slot, h):
        return rdma(zsend.at[k, h], zrecv.at[slot, h], pz_send.at[k, h], pz_recv.at[slot, h], col=to * XN + x)

    @pl.loop(0, (Z - 1) * 2)
    def _(n):
        k, h = lax.div(n, 2), lax.rem(n, 2)
        zd = order(k)
        right = zd > z
        more = jnp.logical_or(jnp.logical_and(right, z > 0), jnp.logical_and(zd < z, z < Z - 1))
        total = x_sum(k, h)

        @pl.when(more)
        def _():
            pz_copy(k, z, zd, h).wait_recv()
            zsend[k, h] = (total + zrecv[zd, h].astype(jnp.float32)).astype(jnp.bfloat16)

        @pl.when(jnp.logical_not(more))
        def _():
            zsend[k, h] = total.astype(jnp.bfloat16)

        to = jnp.where(right, z + 1, z - 1)
        slot = jnp.where(zd == z - 1, Z, zd)
        pz_copy(k, to, slot, h).start()

    for h in range(2):
        mine = pl.ds(h * half, half)
        target[mine, :] = x_sum(Z - 1, h)
        for here, slot in ((z > 0, z), (z < Z - 1, Z)):
            @pl.when(here)
            def _():
                pz_copy(0, z, slot, h).wait_recv()
                target[mine, :] += zrecv[slot, h].astype(jnp.float32)

    for cond, make in sent:
        pl.when(cond)(lambda make=make: make().wait_send())
    groups = [cf, rf] + [cg(e) for e in range(ITERS)] + [rg(e) for e in range(ITERS - 1)]
    for group in groups:
        for copy in put(*group):
            copy.wait_send()
    for k in range(Z):
        for d in range(1, XN):
            for h in range(2):
                px_copy(k, d, h).wait_send()
    for k in range(Z - 1):
        for h in range(2):
            pz_copy(k, z, 0, h).wait_send()


def per_device(R, C, noise_latents, data_latents, noise_sizes, data_sizes):
    rows, wc = noise_latents.shape
    cols, wr = data_latents.shape
    width = wc * C
    XN = C // Z
    f32, bf16 = jnp.float32, jnp.bfloat16
    dma = pltpu.SemaphoreType.DMA
    vmem = pl.BlockSpec(memory_space=pltpu.VMEM)
    anywhere = pl.BlockSpec(memory_space=pl.ANY)
    smem = pl.BlockSpec(memory_space=pltpu.SMEM)
    target, f, g = pl.pallas_call(
        functools.partial(kernel, R, C),
        out_shape=(
            jax.ShapeDtypeStruct((rows, wc), f32),
            jax.ShapeDtypeStruct((1, rows), f32),
            jax.ShapeDtypeStruct((1, cols), f32),
        ),
        in_specs=[anywhere, anywhere, smem, smem],
        out_specs=(vmem, vmem, vmem),
        scratch_shapes=[
            pltpu.VMEM((rows, width), bf16),
            pltpu.VMEM((cols, width), bf16),
            pltpu.VMEM((rows, cols), f32),
            pltpu.VMEM((rows, cols), f32),
            pltpu.VMEM((rows, cols), bf16),
            pltpu.VMEM((rows, T), jnp.int32),
            pltpu.VMEM((rows, T), f32),
            pltpu.VMEM((rows, T), f32),
            pltpu.VMEM((1, cols), f32),
            pltpu.VMEM((1, rows), f32),
            pltpu.VMEM((1, cols), f32),
            pltpu.VMEM((1, rows), f32),
            pltpu.VMEM((Z, 1, cols), f32),
            pltpu.VMEM((1, cols), jnp.int32),
            pltpu.VMEM((1, C, 2, rows), f32),
            pltpu.VMEM((1, R, 2, cols), f32),
            pltpu.VMEM((ITERS, C, 1, rows), f32),
            pltpu.VMEM((ITERS - 1, R, 1, cols), f32),
            pltpu.VMEM((Z, XN - 1, 2, rows // 2, wc), bf16),
            pltpu.VMEM((Z, 2, rows // 2, wc), bf16),
            pltpu.VMEM((Z, XN - 1, 2, rows // 2, wc), bf16),
            pltpu.VMEM((Z - 1, 2, rows // 2, wc), bf16),
            pltpu.VMEM((Z + 1, 2, rows // 2, wc), bf16),
            dma((2,)),
            dma((C, 4)),
            dma((C,)),
            dma((R, PIECES, 3)),
            dma((R, PIECES)),
            dma((1, C - 1)),
            dma((1, C)),
            dma((1, R - 1)),
            dma((1, R)),
            dma((ITERS, C - 1)),
            dma((ITERS, C)),
            dma((ITERS - 1, R - 1)),
            dma((ITERS - 1, R)),
            dma((Z, XN - 1, 2)),
            dma((Z, XN - 1, 2)),
            dma((Z - 1, 2)),
            dma((Z + 1, 2)),
        ],
        compiler_params=pltpu.CompilerParams(
            collective_id=0, has_side_effects=True, vmem_limit_bytes=58 * 1024 * 1024
        ),
        name="sinkhorn",
    )(noise_latents, data_latents, noise_sizes, data_sizes)
    velocity = target - noise_latents.astype(f32)
    return velocity, f.reshape(rows), g.reshape(cols)


def solution(mesh):
    placed = (P("row", "col"), P("col", "row"), P(), P())
    return jax.shard_map(
        functools.partial(per_device, mesh.shape["row"], mesh.shape["col"]),
        mesh=mesh,
        in_specs=placed,
        out_specs=(P("row", "col"), P("row"), P("col")),
        check_vma=False,
    )
```
